256 devices in a mesh: row: 16 (over z, y_hi), col: 16 (over x, y_lo, core).
Axes of the slice: x: 4, y: 4 (y_hi: 2, y_lo: 2; y = y_hi * 2 + y_lo), z: 8, core: 2. Of those that a mesh axis runs over, the one named last changes fastest.
Arguments:
- orbitals: bfloat16 [256, 64000], P(('row', 'col')), may hold values from -6 to 6
- pair_list: int32 [256, 8, 2], P(('row', 'col')), may hold values from 0 to 15, as said below
- pair_count: int32 [256], P(('row', 'col')), may hold values from 1 to 8
Outputs:
- exchange_fields: float32 [256, 64000], P(('row', 'col'))
The draws below stay inside these ranges and needn't reach their ends.
Inputs may be any that keep to these rules, and one draw needn't show every extreme that they name: pair_list[., ., 0] is below 16 and pair_list[., ., 1] below 16.
All inputs are finite; a program needn't handle non-finite values.
Results may differ from the reference program's by a relative error of at most 0.0004.
Values may be sent and summed in bfloat16 or wider, within the bound.
A program may use at most 64 MiB of HBM per device.

```python
import jax
import jax.numpy as jnp
from jax import lax

GX = 40
GRID = 64000
BAND_DEV = 1
PAIRS_DEV = 8
BANDS = 256
BLOCK_R = 16
BLOCK_C = 16
N_COL = 16


def draw_pair_list(key, part):
    key = jax.random.fold_in(key, 11)
    devices = BANDS // BAND_DEV
    key_first, key_second = jax.random.split(key)
    firsts = jax.random.randint(key_first, (devices, PAIRS_DEV), 0, BLOCK_R)
    seconds = jax.random.randint(key_second, (devices, PAIRS_DEV), 0, BLOCK_C)
    firsts = firsts.at[0, 0].set(BLOCK_R - 1).at[0, 1].set(0)
    seconds = seconds.at[0, 0].set(BLOCK_C - 1).at[0, 1].set(0)
    return jnp.stack([firsts, seconds], axis=-1).astype(jnp.int32)


def draw_pair_count(key, part):
    key = jax.random.fold_in(key, 23)
    devices = BANDS // BAND_DEV
    row_total = BANDS // BLOCK_R
    row_numbers = jnp.arange(devices, dtype=jnp.int32) // (BLOCK_R // BAND_DEV)
    jitter = jax.random.randint(key, (devices,), 0, 2)
    counts = jnp.maximum(1, PAIRS_DEV - row_numbers * PAIRS_DEV // row_total - jitter)
    counts = counts.at[0].set(PAIRS_DEV).at[devices - 1].set(1)
    return counts.astype(jnp.int32)


def block_scale(own_key, extent, shards, least, high):
    loudness = 1.0
    for axis_at, parts in shards:
        heights = jax.random.uniform(jax.random.fold_in(jax.random.fold_in(own_key, 6), axis_at), (parts,), jnp.float32, least / len(shards), high / len(shards))
        loudness = loudness * jnp.repeat(jnp.exp(heights), extent[axis_at] // parts).reshape((-1,) + (1,) * (len(extent) - 1 - axis_at))
    return loudness


def centred(key, extent, width, reach, cuts=(), kind=jnp.bfloat16):
    factor_of = block_scale(key, extent, cuts, -0.22, 0.18) if cuts else 1.0
    array = jax.random.normal(key, extent, jnp.float32) * width * factor_of
    return jnp.minimum(jnp.maximum(array, -reach), reach).astype(kind)


def setup_inputs(seed: int = 0) -> dict:
    arg_keys = jax.random.split(jax.random.key(seed), 4)
    return {
        "orbitals": centred(arg_keys[0], (BANDS, GRID), 1.0, 6.0, ((0, 256),)),
        "pair_list": draw_pair_list(jax.random.fold_in(arg_keys[3], 71), 0),
        "pair_count": draw_pair_count(jax.random.fold_in(arg_keys[3], 71), 0),
    }


screen_width = 0.9


def kernel_grid():
    frequency = jnp.fft.fftfreq(GX) * (2.0 * jnp.pi)
    squared = frequency * frequency
    squared_sum = squared[:, None, None] + squared[None, :, None] + squared[None, None, :]
    safe_sum = jnp.where(squared_sum > 0, squared_sum, 1.0)
    screened = 4.0 * jnp.pi * (1.0 - jnp.exp(-safe_sum / (4.0 * screen_width ** 2))) / safe_sum
    return jnp.where(squared_sum > 0, screened, jnp.pi / screen_width ** 2).astype(jnp.float32)


def reference(orbitals, pair_list, pair_count):
    device_ids = jnp.arange(BANDS // BAND_DEV, dtype=jnp.int32)
    row_ids = device_ids // N_COL
    col_ids = device_ids % N_COL
    first_index = row_ids[:, None] * BLOCK_R + pair_list[:, :, 0]
    second_local = pair_list[:, :, 1]
    second_index = ((second_local // BAND_DEV) * N_COL + col_ids[:, None]) * BAND_DEV + second_local % BAND_DEV
    active = (jnp.arange(PAIRS_DEV, dtype=jnp.int32)[None, :] < pair_count[:, None]).astype(jnp.float32)
    mirrored = jnp.where(first_index != second_index, 1.0, 0.0).astype(jnp.float32) * active
    wavefunctions = orbitals.astype(jnp.float32)
    kernel = kernel_grid()

    def add_pair(fields, pair_item):
        first_band, second_band, first_weight, second_weight = pair_item
        first_wave = lax.dynamic_index_in_dim(wavefunctions, first_band, 0, keepdims=False)
        second_wave = lax.dynamic_index_in_dim(wavefunctions, second_band, 0, keepdims=False)
        density = (first_wave * second_wave).reshape(GX, GX, GX)
        spectrum = jnp.fft.fftn(density)
        potential = jnp.real(jnp.fft.ifftn(spectrum * kernel)).reshape(-1).astype(jnp.float32)
        fields = fields.at[first_band].add(first_weight * potential * second_wave)
        fields = fields.at[second_band].add(second_weight * potential * first_wave)
        return fields, None

    fields = jnp.zeros((BANDS, GRID), jnp.float32)
    fields = lax.scan(add_pair, fields, (first_index.reshape(-1), second_index.reshape(-1), active.reshape(-1), mirrored.reshape(-1)))[0]
    return fields
```

```python
import functools

import jax
import jax.numpy as jnp
import ml_dtypes
import numpy as np
from jax import lax
from jax.experimental import pallas as pl
from jax.experimental.pallas import tpu as pltpu
from jax.sharding import PartitionSpec as P

GX = 40
PLANE = GX * GX
LANES = 1664
SLOTS = 8
ROWS = SLOTS * GX
NZ, NX = 8, 4
screen_width = 0.9
MESH = pl.DeviceIdType.MESH
F32, BF16 = jnp.float32, jnp.bfloat16


def split_np(a):
    high = a.astype(ml_dtypes.bfloat16)
    low = (a - high.astype(np.float64)).astype(ml_dtypes.bfloat16)
    return high, low


@functools.cache
def tables():
    n = np.arange(GX)
    phase = 2.0 * np.pi * ((n[:, None] * n[None, :]) % GX) / GX
    hartley = (np.cos(phase) + np.sin(phase)) / np.sqrt(GX)
    plane = np.zeros((LANES, LANES))
    plane[:PLANE, :PLANE] = np.kron(hartley, hartley)
    plane_high, plane_low = split_np(plane)
    high, low = split_np(np.kron(np.eye(2), hartley))
    along = np.concatenate([high, high, low], axis=1)
    signed = np.where(n < GX // 2, n, n - GX) * (2.0 * np.pi / GX)
    squared = signed**2
    total = squared[:, None, None] + squared[None, :, None] + squared[None, None, :]
    safe = np.where(total > 0, total, 1.0)
    screened = 4.0 * np.pi * (1.0 - np.exp(-safe / (4.0 * screen_width**2))) / safe
    kernel = np.where(total > 0, screened, np.pi / screen_width**2).reshape(GX, PLANE)
    padded = np.zeros((GX, LANES), np.float32)
    padded[:, :PLANE] = kernel
    return plane_high, plane_low, along, padded


def split(x):
    high = x.astype(BF16)
    return high, (x - high.astype(F32)).astype(BF16)


def places():
    r, c = lax.axis_index("row"), lax.axis_index("col")
    z, yh = r // 2, r % 2
    x, yl, core = c // 4, (c // 2) % 2, c % 2

    def row_of(dz, y):
        return ((z + dz + NZ) % NZ) * 2 + y

    def col_of(dx, y, k):
        return ((x + dx + NX) % NX) * 4 + y * 2 + k

    ids = {
        "z+": (row_of(1, yh), c),
        "z-": (row_of(-1, yh), c),
        "yh": (row_of(0, 1 - yh), c),
        "x+": (r, col_of(1, yl, core)),
        "x-": (r, col_of(-1, yl, core)),
        "yl": (r, col_of(0, 1 - yl, core)),
        "core": (r, col_of(0, yl, 1 - core)),
    }
    return r, c, yh, yl, core, row_of, col_of, ids


def greet(ids):
    barrier = pltpu.get_barrier_semaphore()
    for device in ids.values():
        pl.semaphore_signal(barrier, inc=1, device_id=device, device_id_type=MESH)
    pl.semaphore_wait(barrier, len(ids))


class Wires:
    def __init__(self, send_sem, recv_sem):
        self.send_sem, self.recv_sem, self.count = send_sem, recv_sem, 0

    def start(self, source, target, device):
        at = self.count
        self.count += 1
        copy = pltpu.make_async_remote_copy(
            src_ref=source,
            dst_ref=target,
            send_sem=self.send_sem.at[at],
            recv_sem=self.recv_sem.at[at],
            device_id=device,
            device_id_type=MESH,
        )
        copy.start()
        return copy


GATHER_COPIES = 30


def gather_kernel(own, col_block, row_block, send_sem, recv_sem, local_sem):
    r, c, yh, yl, core, row_of, col_of, ids = places()
    greet(ids)
    wires = Wires(send_sem, recv_sem)
    copies = []

    def send(block, index, source, where):
        copy = wires.start(source, block.at[index], ids[where])
        copies.append(copy)
        return copy

    local = [
        pltpu.make_async_copy(own, col_block.at[r], local_sem.at[0]),
        pltpu.make_async_copy(own, row_block.at[c], local_sem.at[1]),
    ]
    for copy in local:
        copy.start()
    col_b, row_b = col_block, row_block
    partner = send(col_b, r, own, "yh")
    plus_own = send(col_b, r, own, "z+")
    minus_own = send(col_b, r, own, "z-")
    mate = send(row_b, c, own, "yl")
    x_plus_own = send(row_b, c, own, "x+")
    x_minus_own = send(row_b, c, own, "x-")
    to_core = [send(row_b, c, own, "core")]

    partner.wait_recv()
    other = row_of(0, 1 - yh)
    plus_other = send(col_b, other, col_b.at[other], "z+")
    minus_other = send(col_b, other, col_b.at[other], "z-")
    mate.wait_recv()
    other_c = col_of(0, 1 - yl, core)
    x_plus_other = send(row_b, other_c, row_b.at[other_c], "x+")
    x_minus_other = send(row_b, other_c, row_b.at[other_c], "x-")
    to_core.append(send(row_b, other_c, row_b.at[other_c], "core"))

    def forward_x(first, second, sign, where):
        first.wait_recv()
        mine = col_of(-sign, yl, core)
        to_core.append(send(row_b, mine, row_b.at[mine], "core"))
        second.wait_recv()
        theirs = col_of(-sign, 1 - yl, core)
        to_core.append(send(row_b, theirs, row_b.at[theirs], "core"))
        lane = col_of(-sign, 0 if sign > 0 else 1, core)
        return send(row_b, lane, row_b.at[lane], where)

    def forward_z(first, second, step, sign, where):
        first.wait_recv()
        mine = row_of(-sign * step, yh)
        a = send(col_b, mine, col_b.at[mine], where)
        second.wait_recv()
        theirs = row_of(-sign * step, 1 - yh)
        b = send(col_b, theirs, col_b.at[theirs], where)
        return a, b

    plus = forward_z(plus_own, plus_other, 1, 1, "z+")
    minus = forward_z(minus_own, minus_other, 1, -1, "z-")
    x_far_plus = forward_x(x_plus_own, x_plus_other, 1, "x+")
    x_far_minus = forward_x(x_minus_own, x_minus_other, -1, "x-")
    plus = forward_z(*plus, 2, 1, "z+")
    minus = forward_z(*minus, 2, -1, "z-")
    x_far_plus.wait_recv()
    far = col_of(2, 0, core)
    to_core.append(send(row_b, far, row_b.at[far], "core"))
    x_far_minus.wait_recv()
    far = col_of(2, 1, core)
    to_core.append(send(row_b, far, row_b.at[far], "core"))
    for copy in plus + minus:
        copy.wait_recv()
    far = row_of(-3, 0)
    last_plus = send(col_b, far, col_b.at[far], "z+")
    far = row_of(3, 1)
    last_minus = send(col_b, far, col_b.at[far], "z-")
    for copy in to_core:
        copy.wait_recv()
    last_plus.wait_recv()
    last_minus.wait_recv()
    for copy in copies:
        copy.wait_send()
    for copy in local:
        copy.wait()


TILES = tuple((j * 256, 256) for j in range(6)) + ((1536, 128),)


def over_tiles(body):
    def step(j, carry):
        body(pl.multiple_of(j * 256, 256), 256)
        return carry

    lax.fori_loop(0, LANES // 256, step, 0)
    body(LANES - 128, 128)


def compute_kernel(
    pair_list, pair_count, global_places, col_block, row_block, plane_high, plane_low, along,
    kernel, first_fields, second_fields, density, spectrum, potential
):
    first_fields[...] = jnp.zeros_like(first_fields)
    second_fields[...] = jnp.zeros_like(second_fields)
    row_at, col_at = global_places[0], global_places[1]
    firsts = [pair_list[2 * p] for p in range(SLOTS)]
    seconds = [pair_list[2 * p + 1] for p in range(SLOTS)]
    count = pair_count[0]

    for q in range(SLOTS // 2):
        def wave(p):
            return row_block[firsts[p]].astype(F32) * col_block[seconds[p]].astype(F32)

        both = jnp.concatenate([wave(2 * q), wave(2 * q + 1)], axis=0)
        high, low = split(both)
        density[pl.ds(80 * q, 80), :] = high
        density[pl.ds(ROWS + 80 * q, 80), :] = low

    def plane_product(values, at, width):
        lanes = pl.ds(at, width)
        wide = jnp.dot(values[...], plane_high[:, lanes], preferred_element_type=F32)
        thin = jnp.dot(values[pl.ds(0, ROWS), :], plane_low[:, lanes], preferred_element_type=F32)
        return wide[:ROWS] + wide[ROWS:] + thin

    def along_x(part):
        high, low = split(part)
        stacked = jnp.concatenate([high, low, high], axis=0)
        return jnp.dot(along[...], stacked, preferred_element_type=F32)

    def forward(at, width):
        lanes = pl.ds(at, width)
        turned = plane_product(density, at, width)
        table = kernel[:, lanes]
        table = jnp.concatenate([table, table], axis=0)
        for q in range(SLOTS // 2):
            part = along_x(turned[80 * q : 80 * q + 80]) * table
            high, low = split(along_x(part))
            spectrum[pl.ds(80 * q, 80), lanes] = high
            spectrum[pl.ds(ROWS + 80 * q, 80), lanes] = low

    over_tiles(forward)

    def backward(at, width):
        lanes = pl.ds(at, width)
        potential[:, pl.ds(0, width)] = plane_product(spectrum, at, width)
        for p in range(SLOTS):
            f, s = firsts[p], seconds[p]
            live = jnp.where(p < count, 1.0, 0.0).astype(F32)
            same = (row_at * 16 + f) == (s * 16 + col_at)
            mirrored = jnp.where(same, 0.0, live).astype(F32)
            field = potential[pl.ds(GX * p, GX), pl.ds(0, width)]
            first_fields[f, :, lanes] += (live * field) * col_block[s, :, lanes].astype(F32)
            second_fields[s, :, lanes] += (mirrored * field) * row_block[f, :, lanes].astype(F32)

    over_tiles(backward)


SCATTER_COPIES = 30


def scatter_kernel(first_fields, second_fields, out, sent, received, send_sem, recv_sem):
    r, c, yh, yl, core, row_of, col_of, ids = places()
    greet(ids)
    wires = Wires(send_sem, recv_sem)
    copies = []
    terms = second_fields
    next_sent = [0]

    def send(source, where):
        at = wires.count
        copy = wires.start(source, received.at[at], ids[where])
        copies.append(copy)
        return copy, at

    def arrived(message):
        message[0].wait_recv()
        return received[message[1]]

    def send_value(value, where):
        slot = next_sent[0]
        next_sent[0] += 1
        sent[slot] = value
        return send(sent.at[slot], where)

    m0 = send(terms.at[row_of(4, 0)], "z+")
    n0 = send(terms.at[row_of(-4, 1)], "z-")
    m2 = send(terms.at[row_of(3, 1)], "z+")
    n2 = send(terms.at[row_of(-3, 0)], "z-")
    order = [(2, 0), (2, 1), (1, 0), (1, 1), (-1, 0), (-1, 1), (0, 0), (0, 1)]
    swaps = {
        key: send(first_fields.at[col_of(key[0], key[1], 1 - core)], "core") for key in order
    }

    def chip_sum(key):
        return first_fields[col_of(key[0], key[1], core)] + arrived(swaps[key])

    q0 = send_value(chip_sum((2, 0)), "x+")
    s0 = send_value(chip_sum((2, 1)), "x-")
    q2 = send_value(chip_sum((1, 1)), "x+")
    s2 = send_value(chip_sum((-1, 0)), "x-")
    m1 = send_value(terms[row_of(3, 0)] + arrived(m0), "z+")
    n1 = send_value(terms[row_of(-3, 1)] + arrived(n0), "z-")
    m4 = send_value(terms[row_of(2, 1)] + arrived(m2), "z+")
    n4 = send_value(terms[row_of(-2, 0)] + arrived(n2), "z-")
    q1 = send_value(chip_sum((1, 0)) + arrived(q0), "x+")
    s1 = send_value(chip_sum((-1, 1)) + arrived(s0), "x-")
    m3 = send_value(terms[row_of(2, 0)] + arrived(m1), "z+")
    n3 = send_value(terms[row_of(-2, 1)] + arrived(n1), "z-")
    m6 = send_value(terms[row_of(1, 1)] + arrived(m4), "z+")
    n6 = send_value(terms[row_of(-1, 0)] + arrived(n4), "z-")
    low = sent.shape[0] - 2
    high = sent.shape[0] - 1
    sent[low] = chip_sum((0, 0)) + arrived(q1) + arrived(s2)
    sent[high] = chip_sum((0, 1)) + arrived(q2) + arrived(s1)
    last_x = send(sent.at[low + 1 - yl], "yl")
    m5 = send_value(terms[row_of(1, 0)] + arrived(m3), "z+")
    n5 = send_value(terms[row_of(-1, 1)] + arrived(n3), "z-")
    out[...] = sent[low + yl] + arrived(last_x)
    last_x[0].wait_send()
    sent[low] = terms[row_of(0, 0)] + arrived(m5) + arrived(n6)
    sent[high] = terms[row_of(0, 1)] + arrived(m6) + arrived(n5)
    last_z = send(sent.at[low + 1 - yh], "yh")
    out[...] += sent[low + yh]
    out[...] += arrived(last_z)
    for copy in copies:
        if copy is not last_x[0]:
            copy.wait_send()


def shards(orbitals, pair_list, pair_count):
    vmem = pl.BlockSpec(memory_space=pltpu.VMEM)
    smem = pl.BlockSpec(memory_space=pltpu.SMEM)
    anywhere = pl.BlockSpec(memory_space=pl.ANY)
    plane_high, plane_low, along, kernel = (jnp.asarray(t) for t in tables())
    own = jnp.pad(orbitals.reshape(GX, PLANE), ((0, 0), (0, LANES - PLANE)))
    block = jax.ShapeDtypeStruct((16, GX, LANES), BF16)
    col_block, row_block = pl.pallas_call(
        gather_kernel,
        out_shape=(block, block),
        in_specs=[anywhere],
        out_specs=(anywhere, anywhere),
        scratch_shapes=[
            pltpu.SemaphoreType.DMA((GATHER_COPIES,)),
            pltpu.SemaphoreType.DMA((GATHER_COPIES,)),
            pltpu.SemaphoreType.DMA((2,)),
        ],
        compiler_params=pltpu.CompilerParams(collective_id=0, has_side_effects=True),
        name="gather",
    )(own)
    at = jnp.stack([lax.axis_index("row"), lax.axis_index("col")]).astype(jnp.int32)
    fields = jax.ShapeDtypeStruct((16, GX, LANES), F32)
    first_fields, second_fields = pl.pallas_call(
        compute_kernel,
        out_shape=(fields, fields),
        in_specs=[smem] * 3 + [vmem] * 6,
        out_specs=(vmem, vmem),
        scratch_shapes=[
            pltpu.VMEM((2 * ROWS, LANES), BF16),
            pltpu.VMEM((2 * ROWS, LANES), BF16),
            pltpu.VMEM((ROWS, 256), F32),
        ],
        compiler_params=pltpu.CompilerParams(vmem_limit_bytes=56 * 1024 * 1024),
        name="pairs",
    )(pair_list.reshape(-1), pair_count, at, col_block, row_block, plane_high, plane_low, along, kernel)
    total = pl.pallas_call(
        scatter_kernel,
        out_shape=jax.ShapeDtypeStruct((GX, LANES), F32),
        in_specs=[vmem, vmem],
        out_specs=vmem,
        scratch_shapes=[
            pltpu.VMEM((18, GX, LANES), F32),
            pltpu.VMEM((SCATTER_COPIES, GX, LANES), F32),
            pltpu.SemaphoreType.DMA((SCATTER_COPIES,)),
            pltpu.SemaphoreType.DMA((SCATTER_COPIES,)),
        ],
        compiler_params=pltpu.CompilerParams(
            collective_id=1, has_side_effects=True, vmem_limit_bytes=56 * 1024 * 1024
        ),
        name="scatter",
    )(first_fields, second_fields)
    return total[:, :PLANE].reshape(1, GX * PLANE)


def solution(mesh):
    return jax.shard_map(
        shards,
        mesh=mesh,
        in_specs=(P(("row", "col"), None), P(("row", "col"), None, None), P(("row", "col"))),
        out_specs=P(("row", "col"), None),
        check_vma=False,
    )
```

```python
import functools

import jax
import jax.numpy as jnp
import ml_dtypes
import numpy as np
from jax import lax
from jax.experimental import pallas as pl
from jax.experimental.pallas import tpu as pltpu
from jax.sharding import PartitionSpec as P

GX = 40
HALF = GX // 2
PART = HALF * GX
MAIN = 768
TAIL = PART - MAIN
WIDE = 2 * MAIN + 128
FOLD = MAIN + 128
SLOTS = 8
BANDS = 16
NZ, NX = 8, 4
SLAB_ROWS = (16, 16, 8)
SLAB_LANES = (WIDE, WIDE, FOLD)
SLABS = range(3)
screen_width = 0.9
MESH = pl.DeviceIdType.MESH
F32, BF16, I16 = jnp.float32, jnp.bfloat16, jnp.int16
TOP = 32767.0
GATHER_COPIES = 30
SCATTER_COPIES = 30
CODED = 22


def split_np(a):
    high = a.astype(ml_dtypes.bfloat16)
    low = (a - high.astype(np.float64)).astype(ml_dtypes.bfloat16)
    return high, low


@functools.cache
def tables():
    def cas(phase):
        return np.cos(phase) + np.sin(phase)

    n, h = np.arange(GX), np.arange(HALF)
    root = 1.0 / np.sqrt(GX)
    full = cas(2.0 * np.pi * np.outer(n, n) / GX) * root
    even = cas(2.0 * np.pi * np.outer(h, h) / HALF) * root
    odd = cas(2.0 * np.pi * np.outer(2 * h + 1, 2 * h + 1) / (4 * HALF)) * root
    plane = np.zeros((2, FOLD, FOLD))
    plane[0, :PART, :PART] = np.kron(even, full)
    plane[1, :PART, :PART] = np.kron(odd, full)
    plane_high, plane_low = split_np(plane)
    xs = np.concatenate([np.r_[a:b, a:b] for a, b in ((0, 16), (16, 32), (32, 40))])
    pair = np.concatenate([np.r_[[0] * k, [1] * k] for k in (16, 16, 8)])
    both = np.where(pair[:, None] == pair[None, :], full[xs][:, xs], 0.0)
    high, low = split_np(both)
    along = np.concatenate([high, high, low], axis=1)
    signed = np.where(n < GX // 2, n, n - GX) * (2.0 * np.pi / GX)
    squared = signed**2
    total = squared[:, None, None] + squared[None, :, None] + squared[None, None, :]
    safe = np.where(total > 0, total, 1.0)
    screened = 4.0 * np.pi * (1.0 - np.exp(-safe / (4.0 * screen_width**2))) / safe
    kernel = np.where(total > 0, screened, np.pi / screen_width**2)
    padded = np.zeros((GX, 2, FOLD), np.float32)
    padded[:, 0, :PART] = kernel[:, 0::2].reshape(GX, PART)
    padded[:, 1, :PART] = kernel[:, 1::2].reshape(GX, PART)
    return plane_high, plane_low, along, padded.reshape(GX, 2 * FOLD)[xs]


def split(x):
    high = x.astype(BF16)
    return high, (x - high.astype(F32)).astype(BF16)


def encode(value):
    most = jnp.max(jnp.abs(value), axis=1, keepdims=True)
    power = jnp.floor(jnp.log(jnp.maximum(most, 1e-30)) * 1.4426950408889634)
    share = value * (0.5 * jnp.exp2(-power))
    root = share * lax.rsqrt(jnp.maximum(jnp.abs(share), 1e-20))
    code = jnp.clip(jnp.round(root * TOP), -TOP, TOP)
    lanes = lax.broadcasted_iota(jnp.int32, (value.shape[0], 128), 1)
    last = jnp.where(lanes >= 64, power, code[:, -128:])
    return jnp.concatenate([code[:, :-128], last], axis=1).astype(jnp.int32).astype(I16)


def decode(code):
    wide = code.astype(jnp.int32).astype(F32)
    scale = jnp.exp2(wide[:, -64:-63]) * (2.0 / (TOP * TOP))
    return wide * jnp.abs(wide) * scale


def places():
    r, c = lax.axis_index("row"), lax.axis_index("col")
    z, yh = r // 2, r % 2
    x, yl, core = c // 4, (c // 2) % 2, c % 2

    def row_of(dz, y):
        return ((z + dz + NZ) % NZ) * 2 + y

    def col_of(dx, y, k):
        return ((x + dx + NX) % NX) * 4 + y * 2 + k

    ids = {
        "z+": (row_of(1, yh), c),
        "z-": (row_of(-1, yh), c),
        "yh": (row_of(0, 1 - yh), c),
        "x+": (r, col_of(1, yl, core)),
        "x-": (r, col_of(-1, yl, core)),
        "yl": (r, col_of(0, 1 - yl, core)),
        "core": (r, col_of(0, yl, 1 - core)),
    }
    return r, c, yh, yl, core, row_of, col_of, ids


def greet(ids):
    barrier = pltpu.get_barrier_semaphore()
    for device in ids.values():
        pl.semaphore_signal(barrier, inc=1, device_id=device, device_id_type=MESH)
    pl.semaphore_wait(barrier, len(ids))


class Wires:
    def __init__(self, send_sem, recv_sem, ids):
        self.send_sem, self.recv_sem, self.ids = send_sem, recv_sem, ids
        self.copies = []

    def start(self, source, target, where):
        at = len(self.copies)
        copy = pltpu.make_async_remote_copy(
            src_ref=source,
            dst_ref=target,
            send_sem=self.send_sem.at[at],
            recv_sem=self.recv_sem.at[at],
            device_id=self.ids[where],
            device_id_type=MESH,
        )
        copy.start()
        self.copies.append(copy)
        return copy


def gather_stages(wires, place, own, cols, rows):
    r, c, yh, yl, core, row_of, col_of, _ = place
    got = {}

    def send_col(name, index, where, source=None):
        got[name] = wires.start(cols.at[index] if source is None else source, cols.at[index], where)

    def send_row(name, index, where, source=None):
        got[name] = wires.start(rows.at[index] if source is None else source, rows.at[index], where)

    def stage0():
        send_col("yh", r, "yh", own)
        send_col("z+a", r, "z+", own)
        send_col("z-a", r, "z-", own)
        send_row("yl", c, "yl", own)
        send_row("x+a", c, "x+", own)
        send_row("x-a", c, "x-", own)
        send_row("k0", c, "core", own)

    def stage1():
        got["yh"].wait_recv()
        other = row_of(0, 1 - yh)
        send_col("z+b", other, "z+")
        send_col("z-b", other, "z-")
        got["yl"].wait_recv()
        other = col_of(0, 1 - yl, core)
        send_row("x+b", other, "x+")
        send_row("x-b", other, "x-")
        send_row("k1", other, "core")

    def forward_z(step):
        for sign, where in ((1, "z+"), (-1, "z-")):
            got[where + "a"].wait_recv()
            send_col(where + "a", row_of(-sign * step, yh), where)
        for sign, where in ((1, "z+"), (-1, "z-")):
            got[where + "b"].wait_recv()
            send_col(where + "b", row_of(-sign * step, 1 - yh), where)

    def stage2():
        forward_z(1)
        for sign, where, lane in ((1, "x+", 0), (-1, "x-", 1)):
            got[where + "a"].wait_recv()
            send_row("k2" + where, col_of(-sign, yl, core), "core")
            got[where + "b"].wait_recv()
            send_row("k3" + where, col_of(-sign, 1 - yl, core), "core")
            send_row(where + "c", col_of(-sign, lane, core), where)

    def stage3():
        forward_z(2)
        for where, lane in (("x+", 0), ("x-", 1)):
            got[where + "c"].wait_recv()
            send_row("k4" + where, col_of(2, lane, core), "core")

    def stage4():
        for name in ("z+a", "z-a", "z+b", "z-b"):
            got[name].wait_recv()
        send_col("z+c", row_of(-3, 0), "z+")
        send_col("z-c", row_of(3, 1), "z-")

    def stage5():
        for name in ("z+c", "z-c", "k0", "k1", "k2x+", "k3x+", "k2x-", "k3x-", "k4x+", "k4x-"):
            got[name].wait_recv()

    return [stage0, stage1, stage2, stage3, stage4, stage5]


def scatter_stages(wires, place, first_at, second_at, firsts, seconds, coded, codes_in, swapped, swaps_in, store):
    r, c, yh, yl, core, row_of, col_of, _ = place
    got, used = {}, [0]

    def term(index):
        return seconds[second_at(index)]

    def send(name, value, where):
        slot = used[0]
        used[0] += 1
        coded[slot] = encode(value)
        got[name] = (wires.start(coded.at[slot], codes_in.at[slot], where), slot)

    def arrived(name):
        copy, slot = got[name]
        copy.wait_recv()
        return decode(codes_in[slot])

    order = [(2, 0), (2, 1), (1, 1), (-1, 0), (1, 0), (-1, 1), (0, 0), (0, 1)]

    def stage0():
        send("m0", term(row_of(4, 0)), "z+")
        send("n0", term(row_of(-4, 1)), "z-")
        for slot, (dx, y) in enumerate(order):
            swapped[slot] = firsts[first_at(col_of(dx, y, 1 - core))]
            got[dx, y] = (wires.start(swapped.at[slot], swaps_in.at[slot], "core"), slot)
        send("m2", term(row_of(3, 1)), "z+")
        send("n2", term(row_of(-3, 0)), "z-")

    def chip_sum(key):
        copy, slot = got[key]
        copy.wait_recv()
        return firsts[first_at(col_of(key[0], key[1], core))] + swaps_in[slot]

    def stage1():
        send("q0", chip_sum((2, 0)), "x+")
        send("s0", chip_sum((2, 1)), "x-")
        send("m1", term(row_of(3, 0)) + arrived("m0"), "z+")
        send("n1", term(row_of(-3, 1)) + arrived("n0"), "z-")
        send("q2", chip_sum((1, 1)), "x+")
        send("s2", chip_sum((-1, 0)), "x-")
        send("m4", term(row_of(2, 1)) + arrived("m2"), "z+")
        send("n4", term(row_of(-2, 0)) + arrived("n2"), "z-")

    def stage2():
        send("q1", chip_sum((1, 0)) + arrived("q0"), "x+")
        send("s1", chip_sum((-1, 1)) + arrived("s0"), "x-")
        send("m3", term(row_of(2, 0)) + arrived("m1"), "z+")
        send("n3", term(row_of(-2, 1)) + arrived("n1"), "z-")
        send("m6", term(row_of(1, 1)) + arrived("m4"), "z+")
        send("n6", term(row_of(-1, 0)) + arrived("n4"), "z-")

    def halves(pair, mine):
        swap = jnp.where(mine == 0, 1.0, 0.0).astype(F32)
        keep = 1.0 - swap
        return swap * pair[0] + keep * pair[1], keep * pair[0] + swap * pair[1]

    kept = {}

    def stage3():
        send("m5", term(row_of(1, 0)) + arrived("m3"), "z+")
        send("n5", term(row_of(-1, 1)) + arrived("n3"), "z-")
        pair = [
            chip_sum((0, 0)) + arrived("q1") + arrived("s2"),
            chip_sum((0, 1)) + arrived("q2") + arrived("s1"),
        ]
        mine, other = halves(pair, yl)
        store(mine, False)
        send("x", other, "yl")

    def stage4():
        pair = [
            term(row_of(0, 0)) + arrived("m5") + arrived("n6"),
            term(row_of(0, 1)) + arrived("m6") + arrived("n5"),
        ]
        mine, other = halves(pair, yh)
        store(mine, True)
        send("z", other, "yh")
        store(arrived("x"), True)

    def stage5():
        store(arrived("z"), True)

    return [stage0, stage1, stage2, stage3, stage4, stage5]


def fold(rho, slab):
    rows = SLAB_ROWS[slab]
    if rows == 16:
        near, far, tail = rho[:, :MAIN], rho[:, MAIN : 2 * MAIN], rho[:, 2 * MAIN :]
    else:
        near, far, tail = rho[:rows, :MAIN], rho[rows:, :MAIN], rho[:rows, MAIN:]
    moved = pltpu.roll(tail, 128 - TAIL, 1)
    even = jnp.concatenate([near + far, tail + moved], axis=1)
    return even, jnp.concatenate([near - far, tail - moved], axis=1)


def exchange_kernel(
    own, pair_list, pair_count, plane_high_in, plane_low_in, along, kernel, out,
    own_0, own_1, own_2, cols_0, cols_1, cols_2, rows_0, rows_1, rows_2,
    dens_0, dens_1, dens_2, spec_0, spec_1, spec_2, first_0, first_1, first_2,
    second_0, second_1, second_2, coded_0, coded_1, coded_2, codes_in_0, codes_in_1, codes_in_2,
    swapped_0, swapped_1, swapped_2, swaps_in_0, swaps_in_1, swaps_in_2,
    plane_high, plane_low, send_sem, recv_sem, local_sem,
):
    owns, cols, rows = (own_0, own_1, own_2), (cols_0, cols_1, cols_2), (rows_0, rows_1, rows_2)
    dens, spec = (dens_0, dens_1, dens_2), (spec_0, spec_1, spec_2)
    first_sums, second_sums = (first_0, first_1, first_2), (second_0, second_1, second_2)
    coded, codes_in = (coded_0, coded_1, coded_2), (codes_in_0, codes_in_1, codes_in_2)
    swapped, swaps_in = (swapped_0, swapped_1, swapped_2), (swaps_in_0, swaps_in_1, swaps_in_2)
    place = places()
    r, c, ids = place[0], place[1], place[-1]

    local = [
        pltpu.make_async_copy(plane_high_in, plane_high, local_sem.at[0]),
        pltpu.make_async_copy(plane_low_in, plane_low, local_sem.at[1]),
    ]
    own_0[...] = own[pl.ds(0, 16), :]
    own_1[...] = own[pl.ds(16, 16), :]
    rest = own[pl.ds(32, 8), :].astype(F32)
    low_rows = jnp.concatenate([rest[:, MAIN : 2 * MAIN], jnp.zeros((8, 128), F32)], axis=1)
    high_rows = jnp.concatenate([rest[:, :MAIN], rest[:, 2 * MAIN :]], axis=1)
    own_2[...] = jnp.concatenate([high_rows, low_rows], axis=0).astype(BF16)
    greet(ids)
    wires = Wires(send_sem, recv_sem, ids)
    keeps = []
    for k in SLABS:
        keeps.append(pltpu.make_async_copy(owns[k], cols[k].at[r], local_sem.at[2 + 2 * k]))
        keeps.append(pltpu.make_async_copy(owns[k], rows[k].at[c], local_sem.at[3 + 2 * k]))
    gather = [gather_stages(wires, place, owns[k], cols[k], rows[k]) for k in SLABS]

    firsts = [pair_list[0, p, 0] for p in range(SLOTS)]
    seconds = [pair_list[0, p, 1] for p in range(SLOTS)]
    count = pair_count[0]
    first_band = [jnp.where(p < count, firsts[p], -1) for p in range(SLOTS)]
    second_band = [
        jnp.where((p < count) & (r * BANDS + firsts[p] != seconds[p] * BANDS + c), seconds[p], -1)
        for p in range(SLOTS)
    ]

    def last_slot(bands, wanted):
        at = SLOTS
        for p, band in enumerate(bands):
            at = jnp.where(band == wanted, p, at)
        return at

    before_first = [last_slot(first_band[:p], first_band[p]) for p in range(SLOTS)]
    before_second = [last_slot(second_band[:p], second_band[p]) for p in range(SLOTS)]

    def density(k, p):
        return rows[k][firsts[p]].astype(F32) * cols[k][seconds[p]].astype(F32)

    def fill(k, slots):
        size = SLAB_ROWS[k]
        group = 16 // size
        for p in range(slots[0], slots[1], group):
            parts = [fold(density(k, p + i), k) for i in range(group)]
            for parity in range(2):
                value = jnp.concatenate([part[parity] for part in parts], axis=0)
                high, low = split(value)
                dens[k][parity, pl.ds(p * size, 16), :] = high
                dens[k][parity, pl.ds((SLOTS + p) * size, 16), :] = low

    def product(values, parity, at, width):
        lanes = pl.ds(at, width)
        half = values.shape[0] // 2
        wide = jnp.dot(values, plane_high[parity, :, lanes], preferred_element_type=F32)
        thin = jnp.dot(values[:half], plane_low[parity, :, lanes], preferred_element_type=F32)
        return wide[:half] + wide[half:] + thin

    def forward(k, parity, at, width):
        size = SLOTS * SLAB_ROWS[k]
        high, low = split(product(dens[k][parity], parity, at, width))
        lanes = pl.ds(parity * FOLD + at, width)
        spec[k][pl.ds(0, size), lanes] = high
        spec[k][pl.ds(size, size), lanes] = low

    def forward_pieces(k):
        pieces = [functools.partial(fill, k, (0, 4)), functools.partial(fill, k, (4, 8))]
        for parity in range(2):
            for at, width in ((0, 512), (512, 384)):
                pieces.append(functools.partial(forward, k, parity, at, width))
        return pieces

    def along_x(part):
        high, low = split(part)
        return jnp.dot(along[...], jnp.concatenate([high, low, high], axis=0), preferred_element_type=F32)

    def middle(j, carry):
        lanes = pl.ds(pl.multiple_of(j * 256, 256), 256)
        table = kernel[:, lanes]
        for q in range(SLOTS // 2):
            def rows_of(shift):
                return [spec[k][pl.ds((shift * SLOTS + 2 * q) * SLAB_ROWS[k], 2 * SLAB_ROWS[k]), lanes] for k in SLABS]

            high, low = rows_of(0), rows_of(1)
            turned = jnp.dot(along[...], jnp.concatenate(high + low + high, axis=0), preferred_element_type=F32)
            high, low = split(along_x(turned * table))
            at = 0
            for k in SLABS:
                size = 2 * SLAB_ROWS[k]
                spec[k][pl.ds(q * size, size), lanes] = high[at : at + size]
                spec[k][pl.ds(SLOTS * SLAB_ROWS[k] + q * size, size), lanes] = low[at : at + size]
                at += size
        return carry

    def backward(k, at, width):
        size = SLAB_ROWS[k]
        even = product(spec[k][:, pl.ds(0, FOLD)], 0, at, width)
        odd = product(spec[k][:, pl.ds(FOLD, FOLD)], 1, at, width)
        near, far = even + odd, even - odd
        if at == MAIN:
            lane = lax.broadcasted_iota(jnp.int32, near.shape, 1)
            near = jnp.where(lane < TAIL, near, pltpu.roll(far, TAIL, 1))
        for p in range(SLOTS):
            mine = slice(p * size, (p + 1) * size)
            if at == MAIN:
                spans = [(WIDE - 128 if size == 16 else MAIN, near[mine])]
                if size < 16:
                    spans = [(MAIN, jnp.concatenate([near[mine], jnp.zeros_like(near[mine])], axis=0))]
            elif size == 16:
                spans = [(at, near[mine]), (MAIN + at, far[mine])]
            else:
                spans = [(at, jnp.concatenate([near[mine], far[mine]], axis=0))]
            for start, value in spans:
                lanes = pl.ds(start, width)
                to_first = value * cols[k][seconds[p], :, lanes].astype(F32)
                to_second = value * rows[k][firsts[p], :, lanes].astype(F32)
                first_sums[k][p, :, lanes] = to_first + first_sums[k][before_first[p], :, lanes]
                second_sums[k][p, :, lanes] = to_second + second_sums[k][before_second[p], :, lanes]

    def backward_pieces(k):
        return [functools.partial(backward, k, at, width) for at, width in ((0, 256), (256, 256), (512, 256), (768, 128))]

    def store(k, value, more):
        if SLAB_ROWS[k] == 16:
            spans = [(slice(16 * k, 16 * k + 16), slice(0, WIDE), value)]
        else:
            spans = [
                (slice(32, 40), slice(0, MAIN), value[:8, :MAIN]),
                (slice(32, 40), slice(MAIN, 2 * MAIN), value[8:, :MAIN]),
                (slice(32, 40), slice(2 * MAIN, WIDE), value[:8, MAIN:]),
            ]
        for some_rows, lanes, part in spans:
            out[some_rows, lanes] = out[some_rows, lanes] + part if more else part

    scatter = [
        scatter_stages(
            wires, place, functools.partial(last_slot, first_band), functools.partial(last_slot, second_band),
            first_sums[k], second_sums[k], coded[k], codes_in[k], swapped[k], swaps_in[k],
            functools.partial(store, k),
        )
        for k in SLABS
    ]

    def run(steps):
        for step in steps:
            step()

    def mixed(pieces, stages):
        done = 0
        for i, piece in enumerate(pieces):
            piece()
            while done * len(pieces) < (i + 1) * len(stages) and done < len(stages):
                stages[done]()
                done += 1

    a, b, d = gather
    a[0]()
    for copy in keeps:
        copy.start()
    b[0]()
    for copy in local:
        copy.start()
    run([a[1], d[0], a[2], b[1], a[3], b[2], a[4], d[1], b[3]])
    for k in SLABS:
        first_sums[k][SLOTS] = jnp.zeros(first_sums[k].shape[1:], F32)
        second_sums[k][SLOTS] = jnp.zeros(second_sums[k].shape[1:], F32)
    run([d[2], a[5]])
    for copy in local:
        copy.wait()
    for copy in keeps:
        copy.wait()
    mixed(forward_pieces(0), [b[4], d[3], d[4]])
    b[5]()
    mixed(forward_pieces(1), [])
    d[5]()
    mixed(forward_pieces(2), [])
    lax.fori_loop(0, 2 * FOLD // 256, middle, 0)
    a, b, d = scatter
    run(backward_pieces(0))
    a[0]()
    mixed(backward_pieces(1), [a[1]])
    b[0]()
    mixed(backward_pieces(2), [a[2], b[1]])
    run([d[0], a[3], b[2], d[1], a[4], b[3], d[2], a[5], b[4], d[3], b[5], d[4], d[5]])
    for copy in wires.copies:
        copy.wait_send()


def exchange(own, pair_list, pair_count):
    vmem = pl.BlockSpec(memory_space=pltpu.VMEM)
    smem = pl.BlockSpec(memory_space=pltpu.SMEM)
    anywhere = pl.BlockSpec(memory_space=pl.ANY)
    plane_high, plane_low, along, kernel = (jnp.asarray(t) for t in tables())

    def each(shape, kind):
        return [pltpu.VMEM(shape(k), kind) for k in SLABS]

    def stack(count):
        return lambda k: (count, 16, SLAB_LANES[k])

    copies = len(SLAB_ROWS) * (GATHER_COPIES + SCATTER_COPIES)
    return pl.pallas_call(
        exchange_kernel,
        out_shape=jax.ShapeDtypeStruct((GX, WIDE), F32),
        in_specs=[vmem, smem, smem, anywhere, anywhere, vmem, vmem],
        out_specs=vmem,
        scratch_shapes=[
            *each(lambda k: (16, SLAB_LANES[k]), BF16),
            *each(stack(BANDS), BF16),
            *each(stack(BANDS), BF16),
            *each(lambda k: (2, 2 * SLOTS * SLAB_ROWS[k], FOLD), BF16),
            *each(lambda k: (2 * SLOTS * SLAB_ROWS[k], 2 * FOLD), BF16),
            *each(stack(SLOTS + 1), F32),
            *each(stack(SLOTS + 1), F32),
            *each(stack(CODED), I16),
            *each(stack(CODED), I16),
            *each(stack(SLOTS), F32),
            *each(stack(SLOTS), F32),
            pltpu.VMEM(plane_high.shape, BF16),
            pltpu.VMEM(plane_low.shape, BF16),
            pltpu.SemaphoreType.DMA((copies,)),
            pltpu.SemaphoreType.DMA((copies,)),
            pltpu.SemaphoreType.DMA((8,)),
        ],
        compiler_params=pltpu.CompilerParams(
            collective_id=0, has_side_effects=True, vmem_limit_bytes=52 * 1024 * 1024
        ),
        name="exchange",
    )(own, pair_list, pair_count, plane_high, plane_low, along, kernel)


def shards(orbitals, pair_list, pair_count):
    halves = orbitals.reshape(GX, 2, PART)
    own = jnp.concatenate(
        [halves[:, 0, :MAIN], halves[:, 1, :MAIN], halves[:, 0, MAIN:], halves[:, 1, MAIN:], jnp.zeros((GX, 64), BF16)],
        axis=1,
    )
    fields = exchange(own, pair_list, pair_count)
    near = [fields[:, :MAIN], fields[:, 2 * MAIN : 2 * MAIN + TAIL]]
    far = [fields[:, MAIN : 2 * MAIN], fields[:, 2 * MAIN + TAIL : 2 * MAIN + 2 * TAIL]]
    return jnp.concatenate(near + far, axis=1).reshape(1, GX * GX * GX)


def solution(mesh):
    return jax.shard_map(
        shards,
        mesh=mesh,
        in_specs=(P(("row", "col"), None), P(("row", "col"), None, None), P(("row", "col"))),
        out_specs=P(("row", "col"), None),
        check_vma=False,
    )
```

```python
import functools

import jax
import jax.numpy as jnp
import ml_dtypes
import numpy as np
from jax import lax
from jax.experimental import pallas as pl
from jax.experimental.pallas import tpu as pltpu
from jax.sharding import PartitionSpec as P

GX = 40
HALF = GX // 2
PART = HALF * GX
MAIN = 768
TAIL = PART - MAIN
WIDE = 2 * MAIN + 128
FOLD = MAIN + 128
SLOTS = 8
BANDS = 16
NZ, NX = 8, 4
SLAB_ROWS = (16, 16, 8)
SLAB_LANES = (WIDE, WIDE, FOLD)
SLABS = range(3)
screen_width = 0.9
MESH = pl.DeviceIdType.MESH
F32, BF16, I16 = jnp.float32, jnp.bfloat16, jnp.int16
TOP = 32767.0
Z_FIRST = (False, True, False)
ACROSS = False
FAR_ACROSS = False
COPIES = 192
CODED = 22
GREETED = ("z+", "z-", "yh", "x+", "x-", "yl", "core")


def split_np(a):
    high = a.astype(ml_dtypes.bfloat16)
    low = (a - high.astype(np.float64)).astype(ml_dtypes.bfloat16)
    return high, low


@functools.cache
def tables():
    def cas(phase):
        return np.cos(phase) + np.sin(phase)

    n, h = np.arange(GX), np.arange(HALF)
    root = 1.0 / np.sqrt(GX)
    full = cas(2.0 * np.pi * np.outer(n, n) / GX) * root
    even = cas(2.0 * np.pi * np.outer(h, h) / HALF) * root
    odd = cas(2.0 * np.pi * np.outer(2 * h + 1, 2 * h + 1) / (4 * HALF)) * root
    plane = np.zeros((2, FOLD, FOLD))
    plane[0, :PART, :PART] = np.kron(even, full)
    plane[1, :PART, :PART] = np.kron(odd, full)
    plane_high, plane_low = split_np(plane)
    xs = np.concatenate([np.r_[a:b, a:b] for a, b in ((0, 16), (16, 32), (32, 40))])
    pair = np.concatenate([np.r_[[0] * k, [1] * k] for k in (16, 16, 8)])
    both = np.where(pair[:, None] == pair[None, :], full[xs][:, xs], 0.0)
    high, low = split_np(both)
    along = np.concatenate([high, high, low], axis=1)
    signed = np.where(n < GX // 2, n, n - GX) * (2.0 * np.pi / GX)
    squared = signed**2
    total = squared[:, None, None] + squared[None, :, None] + squared[None, None, :]
    safe = np.where(total > 0, total, 1.0)
    screened = 4.0 * np.pi * (1.0 - np.exp(-safe / (4.0 * screen_width**2))) / safe
    kernel = np.where(total > 0, screened, np.pi / screen_width**2)
    padded = np.zeros((GX, 2, FOLD), np.float32)
    padded[:, 0, :PART] = kernel[:, 0::2].reshape(GX, PART)
    padded[:, 1, :PART] = kernel[:, 1::2].reshape(GX, PART)
    sheet = np.zeros((4 * FOLD + 80, FOLD), ml_dtypes.bfloat16)
    sheet[: 2 * FOLD] = plane_high.reshape(2 * FOLD, FOLD)
    sheet[2 * FOLD : 4 * FOLD] = plane_low.reshape(2 * FOLD, FOLD)
    sheet[4 * FOLD :, :240] = along
    return sheet, np.tile(padded.reshape(GX, 2 * FOLD)[xs], (12, 1))


def split(x):
    high = x.astype(BF16)
    return high, (x - high.astype(F32)).astype(BF16)


def encode(value):
    most = jnp.max(jnp.abs(value), axis=1, keepdims=True)
    power = jnp.floor(jnp.log(jnp.maximum(most, 1e-30)) * 1.4426950408889634)
    share = value * (0.5 * jnp.exp2(-power))
    root = share * lax.rsqrt(jnp.maximum(jnp.abs(share), 1e-20))
    code = jnp.clip(jnp.round(root * TOP), -TOP, TOP)
    lanes = lax.broadcasted_iota(jnp.int32, (value.shape[0], 128), 1)
    last = jnp.where(lanes >= 64, power, code[:, -128:])
    return jnp.concatenate([code[:, :-128], last], axis=1).astype(jnp.int32).astype(I16)


def decode(code):
    wide = code.astype(jnp.int32).astype(F32)
    scale = jnp.exp2(wide[:, -64:-63]) * (2.0 / (TOP * TOP))
    return wide * jnp.abs(wide) * scale


def places():
    r, c = lax.axis_index("row"), lax.axis_index("col")
    z, yh = r // 2, r % 2
    x, yl, core = c // 4, (c // 2) % 2, c % 2

    def row_of(dz, y):
        return ((z + dz + NZ) % NZ) * 2 + y

    def col_of(dx, y, k):
        return ((x + dx + NX) % NX) * 4 + y * 2 + k

    ids = {
        "z+": (row_of(1, yh), c),
        "z-": (row_of(-1, yh), c),
        "zf": (row_of(1 - 2 * core, yh), c),
        "zg": (row_of(2 * core - 1, yh), c),
        "zy+": (row_of(1, 1 - yh), c),
        "zy-": (row_of(-1, 1 - yh), c),
        "zyf": (row_of(1 - 2 * core, 1 - yh), c),
        "yh": (row_of(0, 1 - yh), c),
        "x+": (r, col_of(1, yl, core)),
        "x-": (r, col_of(-1, yl, core)),
        "yl": (r, col_of(0, 1 - yl, core)),
        "core": (r, col_of(0, yl, 1 - core)),
    }
    return r, c, yh, yl, core, row_of, col_of, ids


def place_sign(core):
    return 1 - 2 * core


def greet(ids):
    barrier = pltpu.get_barrier_semaphore()
    for where in GREETED:
        pl.semaphore_signal(barrier, inc=1, device_id=ids[where], device_id_type=MESH)


def met():
    pl.semaphore_wait(pltpu.get_barrier_semaphore(), len(GREETED))


class Wires:
    def __init__(self, send_sem, recv_sem, ids):
        self.send_sem, self.recv_sem, self.ids = send_sem, recv_sem, ids
        self.copies, self.waited = {}, set()

    def start(self, name, source, target, where):
        at = len(self.copies)
        copy = pltpu.make_async_remote_copy(
            src_ref=source,
            dst_ref=target,
            send_sem=self.send_sem.at[at],
            recv_sem=self.recv_sem.at[at],
            device_id=self.ids[where],
            device_id_type=MESH,
        )
        copy.start()
        self.copies[name] = copy

    def arrive(self, name):
        if name not in self.waited:
            self.waited.add(name)
            self.copies[name].wait_recv()


RATES = {"z": 1 / 49e3, "x": 1 / 49e3, "y": 1 / 49e3, "l": 1 / 49e3, "c": 1 / 400e3}
DELAYS = {"z": 2.6, "x": 2.6, "y": 3.5, "l": 2.6, "c": 0.7}


class Task:
    def __init__(self, name, needs, cost, body, emits=(), urgent=True):
        self.name, self.needs, self.cost, self.body = name, list(needs), cost, body
        self.emits, self.urgent = list(emits), urgent


def in_order(tasks):
    known, free, left, order, now = {}, {}, list(tasks), [], 0.0
    while left:
        ready = []
        for rank, task in enumerate(left):
            if all(need in known for need in task.needs):
                at = max([known[need] for need in task.needs], default=0.0)
                ready.append((max(at, now), not task.urgent, at, rank))
        at, _, _, rank = min(ready)
        task = left.pop(rank)
        now = at + task.cost
        known[task.name] = now
        for message, link, size in task.emits:
            begin = max(now, *(free.get(part, 0.0) for part in link))
            for part in link:
                free[part] = begin + size * RATES[part[0]]
            known[message] = free[link[0]] + DELAYS[link[0][0]] + 2.0 * (len(link) - 1)
        task.needs.sort(key=known.get)
        order.append(task)
    return order, now


LINKS = {
    "z+": ("z+",), "z-": ("z-",), "zf": ("z+",), "zg": ("z-",), "zy+": ("z+", "y"), "zy-": ("z-", "y"), "zyf": ("z+", "y"),
    "x+": ("x+",), "x-": ("x-",), "yh": ("y",), "yl": ("l",), "core": ("c",),
}


def gather_tasks(wires, place, k, own, cols, rows):
    r, c, yh, yl, core, row_of, col_of, _ = place
    size = 16 * SLAB_LANES[k] * 2
    tasks = []
    messages = []

    def task(name, needs, sends):
        def body():
            for message, where, block, index, source in sends:
                target = block.at[index]
                wires.start(f"{message}{k}", target if source is None else source, target, where)

        emits = [(f"{send[0]}{k}", LINKS[send[1]], size) for send in sends]
        messages.extend(send[0] for send in sends)
        tasks.append(Task(f"gather {name}{k}", [f"{need}{k}" for need in needs], 0.03 * len(sends), body, emits))

    x_first = [("x+a0", "x+", rows, c, own), ("x-a0", "x-", rows, c, own), ("yl", "yl", rows, c, own), ("k0", "core", rows, c, own)]
    if Z_FIRST[k]:
        sign = place_sign(core)
        task("own", [], [("fa0", "zf", cols, r, own), ("ga0", "zg", cols, r, own), ("y0", "yh", cols, r, own), *x_first])
        for way, turn in (("f", -1), ("g", 1)):
            for step in range(3):
                index = row_of(turn * sign * (step + 1), yh)
                sends = [(f"{way}a{step + 1}", "z" + way, cols, index, None)] if step < (3 if way == "f" else 2) else []
                if FAR_ACROSS and way == "f" and step == 2:
                    sends.append(("yf3", "zyf", cols, index, None))
                task(f"{way}{step}", [f"{way}a{step}"], [*sends, (f"y{way}{step}", "yh", cols, index, None)])
        if not FAR_ACROSS:
            task("far", ["fa3"], [("yf3", "yh", cols, row_of(4, yh), None)])
    else:
        beside = [("z+a0", "z+", cols, r, own), ("z-a0", "z-", cols, r, own)]
        across = [("z+b0", "zy+", cols, r, own), ("z-b0", "zy-", cols, r, own)]
        if ACROSS:
            task("own", [], [*beside, *across, *x_first, ("y0", "yh", cols, r, own)])
        else:
            task("own", [], [*beside, ("y0", "yh", cols, r, own), *x_first])
            other = row_of(0, 1 - yh)
            task("y", ["y0"], [("z+b0", "z+", cols, other, None), ("z-b0", "z-", cols, other, None)])
        for where, turn, long in (("z+", -1, "a"), ("z-", 1, "b")):
            for which, y in (("a", yh), ("b", 1 - yh)):
                for step in range(3 if which == long else 2):
                    index = row_of(turn * (step + 1), y)
                    task(f"{where}{which}{step}", [f"{where}{which}{step}"], [(f"{where}{which}{step + 1}", where, cols, index, None)])
    other = col_of(0, 1 - yl, core)
    task("l", ["yl"], [("x+b0", "x+", rows, other, None), ("x-b0", "x-", rows, other, None), ("k1", "core", rows, other, None)])
    for where, turn, long in (("x+", -1, "a"), ("x-", 1, "b")):
        for which, y in (("a", yl), ("b", 1 - yl)):
            index = col_of(turn, y, core)
            sends = [(f"{where}{which}1", where, rows, index, None)] if which == long else []
            task(f"{where}{which}", [f"{where}{which}0"], [*sends, (f"k{where}{which}0", "core", rows, index, None)])
        index = col_of(2, yl if long == "a" else 1 - yl, core)
        task(f"{where}far", [f"{where}{long}1"], [(f"k{where}far", "core", rows, index, None)])
    return tasks, [f"{message}{k}" for message in messages]


def scatter_tasks(wires, place, k, first_at, second_at, firsts, seconds, coded, codes_in, swapped, swaps_in, store):
    r, c, yh, yl, core, row_of, col_of, _ = place
    size = 16 * SLAB_LANES[k] * 2
    weight = SLAB_LANES[k] / WIDE
    tasks, slots = [], {}

    def term(index):
        return seconds[second_at(index)]

    def arrived(message):
        return decode(codes_in[slots[message]])

    def total(value, needs):
        for need in needs:
            value = value + arrived(need)
        return value

    def send(message, where, value, needs, after=()):
        slots[message] = len(slots)

        def body():
            slot = slots[message]
            coded[slot] = encode(total(value(), needs))
            wires.start(f"{message}/{k}", coded.at[slot], codes_in.at[slot], where)

        needed = [f"{need}/{k}" for need in (*needs, *after)] + [f"backward{k}"]
        cost = 0.03 + weight * (0.08 + 0.02 * len(needs))
        tasks.append(Task(f"scatter {message}{k}", needed, cost, body, [(f"{message}/{k}", LINKS[where], size)]))

    def keep(name, value, needs, after=()):
        def body():
            store(total(value(), needs))

        needed = [f"{need}/{k}" for need in (*needs, *after)] + [f"backward{k}"]
        tasks.append(Task(f"keep {name}{k}", needed, 0.04 * weight, body, urgent=False))

    def of(index):
        return functools.partial(term, index)

    order = [(2, "a"), (2, "b"), (1, "b"), (-1, "a"), (1, "a"), (-1, "b"), (0, "b"), (0, "a")]
    y_of = {"a": yl, "b": 1 - yl}

    def swap_all(some):
        def body():
            for slot in some:
                dx, y = order[slot]
                swapped[slot] = firsts[first_at(col_of(dx, y_of[y], 1 - core))]
                wires.start(f"swap{dx}{y}/{k}", swapped.at[slot], swaps_in.at[slot], "core")

        emits = [(f"swap{order[slot][0]}{order[slot][1]}/{k}", LINKS["core"], 2 * size) for slot in some]
        tasks.append(Task(f"swap{some[0]}{k}", [f"backward{k}"], 0.04 * len(some), body, emits))

    def chip_sum(dx, y):
        return firsts[first_at(col_of(dx, y_of[y], core))] + swaps_in[order.index((dx, y))]

    def of_chip(dx, y):
        return functools.partial(chip_sum, dx, y)

    if Z_FIRST[k]:
        sign = place_sign(core)
        spots = {"f3": 4, "f2": 3 * sign, "g2": -3 * sign, "f1": 2 * sign, "g1": -2 * sign, "f0": sign, "g0": -sign, "0": 0}
        if FAR_ACROSS:
            send("pf3", "zf", of(row_of(4, yh)), ())
        for i, (spot, dz) in enumerate(spots.items()):
            send(f"y{spot}", "zyf" if FAR_ACROSS and i == 0 else "yh", of(row_of(dz, 1 - yh)), ())
            if i == 1:
                swap_all(range(0, 4))
            if i == 3:
                swap_all(range(4, 8))
        if not FAR_ACROSS:
            send("pf3", "zf", of(row_of(4, yh)), ("yf3",))
        for spot, needs in (("f2", ("pf3", "yf3") if FAR_ACROSS else ("pf3",)), ("g2", ()), ("f1", ("pf2",)), ("g1", ("pg2",)), ("f0", ("pf1",)), ("g0", ("pg1",))):
            send(f"p{spot}", "z" + spot[0], of(row_of(spots[spot], yh)), (f"y{spot}", *needs))
        keep("z", of(row_of(0, yh)), ("y0", "pf0", "pg0"))
    else:
        y_row = {"a": yh, "b": 1 - yh}

        def chain(where, turn, which, distance, needs):
            way = "zy" + where[1] if ACROSS and which == "b" and distance == 1 else where
            send(f"p{where}{which}{distance}", way, of(row_of(turn * distance, y_row[which])), needs)

        chain("z+", 1, "a", 4, ())
        chain("z-", -1, "b", 4, ())
        swap_all(range(0, 4))
        chain("z+", 1, "b", 3, ())
        chain("z-", -1, "a", 3, ())
        swap_all(range(4, 8))
        for where, turn, long in (("z+", 1, "a"), ("z-", -1, "b")):
            for which in "ab":
                for distance in range(3 if which == long else 2, 0, -1):
                    chain(where, turn, which, distance, (f"p{where}{which}{distance + 1}",))
        direct = ("pz+b1", "pz-b1")
        send("yb", "yh", of(row_of(0, 1 - yh)), () if ACROSS else direct)
        keep("z", of(row_of(0, yh)), ("pz+a1", "pz-a1", "yb", *(direct if ACROSS else ())))
    send("qx+a2", "x+", of_chip(2, "a"), (), ("swap2a",))
    send("qx-b2", "x-", of_chip(2, "b"), (), ("swap2b",))
    send("qx+b1", "x+", of_chip(1, "b"), (), ("swap1b",))
    send("qx-a1", "x-", of_chip(-1, "a"), (), ("swap-1a",))
    send("qx+a1", "x+", of_chip(1, "a"), ("qx+a2",), ("swap1a",))
    send("qx-b1", "x-", of_chip(-1, "b"), ("qx-b2",), ("swap-1b",))
    send("lb", "yl", of_chip(0, "b"), ("qx+b1", "qx-b1"), ("swap0b",))
    keep("x", of_chip(0, "a"), ("qx+a1", "qx-a1", "lb"), ("swap0a",))
    return tasks


def fold(rho, slab):
    rows = SLAB_ROWS[slab]
    if rows == 16:
        near, far, tail = rho[:, :MAIN], rho[:, MAIN : 2 * MAIN], rho[:, 2 * MAIN :]
    else:
        near, far, tail = rho[:rows, :MAIN], rho[rows:, :MAIN], rho[:rows, MAIN:]
    moved = pltpu.roll(tail, 128 - TAIL, 1)
    even = jnp.concatenate([near + far, tail + moved], axis=1)
    return even, jnp.concatenate([near - far, tail - moved], axis=1)


def exchange_kernel(
    own_in, pair_list_in, pair_count_in, sheet_in, kernel_in, out,
    own, pair_list, pair_count, own_0, own_1, own_2, cols_0, cols_1, cols_2, rows_0, rows_1, rows_2,
    dens_0, dens_1, dens_2, spec_0, spec_1, spec_2, first_0, first_1, first_2,
    second_0, second_1, second_2, coded_0, coded_1, coded_2, codes_in_0, codes_in_1, codes_in_2,
    swapped_0, swapped_1, swapped_2, swaps_in_0, swaps_in_1, swaps_in_2,
    kept_0, kept_1, kept_2, sheet, kernel, send_sem, recv_sem, local_sem,
):
    owns, cols, rows = (own_0, own_1, own_2), (cols_0, cols_1, cols_2), (rows_0, rows_1, rows_2)
    dens, spec = (dens_0, dens_1, dens_2), (spec_0, spec_1, spec_2)
    first_sums, second_sums = (first_0, first_1, first_2), (second_0, second_1, second_2)
    coded, codes_in = (coded_0, coded_1, coded_2), (codes_in_0, codes_in_1, codes_in_2)
    kept = (kept_0, kept_1, kept_2)
    swapped, swaps_in = (swapped_0, swapped_1, swapped_2), (swaps_in_0, swaps_in_1, swaps_in_2)
    place = places()
    r, c, ids = place[0], place[1], place[-1]

    local = [
        pltpu.make_async_copy(sheet_in, sheet, local_sem.at[0]),
        pltpu.make_async_copy(kernel_in.at[pl.ds(0, 80)], kernel, local_sem.at[1]),
        pltpu.make_async_copy(pair_list_in, pair_list, local_sem.at[2]),
        pltpu.make_async_copy(pair_count_in, pair_count, local_sem.at[3]),
    ]
    greet(ids)
    take = pltpu.make_async_copy(own_in, own, local_sem.at[10])
    take.start()
    take.wait()
    for k in SLABS:
        size = SLAB_ROWS[k]
        band = own[pl.ds(16 * k, size), :].astype(F32)
        tails = [band[:, MAIN:PART], band[:, PART + MAIN :], jnp.zeros((size, 128 - 2 * TAIL), F32)]
        near, far, tail = band[:, :MAIN], band[:, PART : PART + MAIN], jnp.concatenate(tails, axis=1)
        if size == 16:
            owns[k][...] = jnp.concatenate([near, far, tail], axis=1).astype(BF16)
        else:
            low_rows = jnp.concatenate([far, jnp.zeros((size, 128), F32)], axis=1)
            owns[k][...] = jnp.concatenate([jnp.concatenate([near, tail], axis=1), low_rows], axis=0).astype(BF16)
    met()
    wires = Wires(send_sem, recv_sem, ids)
    keeps = []
    for k in SLABS:
        keeps.append(pltpu.make_async_copy(owns[k], cols[k].at[r], local_sem.at[4 + 2 * k]))
        keeps.append(pltpu.make_async_copy(owns[k], rows[k].at[c], local_sem.at[5 + 2 * k]))

    firsts, seconds, first_band, second_band, before_first, before_second = [], [], [], [], [], []

    def last_slot(bands, wanted):
        at = SLOTS
        for p, band in enumerate(bands):
            at = jnp.where(band == wanted, p, at)
        return at

    def read_pairs():
        count = pair_count[0]
        for p in range(SLOTS):
            first, second = pair_list[0, 0, p], pair_list[0, 1, p]
            other = r * BANDS + first != second * BANDS + c
            firsts.append(first)
            seconds.append(second)
            first_band.append(jnp.where(p < count, first, -1))
            second_band.append(jnp.where((p < count) & other, second, -1))
            before_first.append(last_slot(first_band[:p], first_band[p]))
            before_second.append(last_slot(second_band[:p], second_band[p]))

    def density(k, p):
        return rows[k][firsts[p]].astype(F32) * cols[k][seconds[p]].astype(F32)

    def fill(k, slots):
        size = SLAB_ROWS[k]
        group = 16 // size
        for p in range(slots[0], slots[1], group):
            parts = [fold(density(k, p + i), k) for i in range(group)]
            for parity in range(2):
                value = jnp.concatenate([part[parity] for part in parts], axis=0)
                high, low = split(value)
                dens[k][parity, pl.ds(p * size, 16), :] = high
                dens[k][parity, pl.ds((SLOTS + p) * size, 16), :] = low

    def product(values, parity, at, width):
        lanes = pl.ds(at, width)
        half = values.shape[0] // 2
        wide = jnp.dot(values, sheet[pl.ds(parity * FOLD, FOLD), lanes], preferred_element_type=F32)
        thin = jnp.dot(values[:half], sheet[pl.ds((2 + parity) * FOLD, FOLD), lanes], preferred_element_type=F32)
        return wide[:half] + wide[half:] + thin

    def forward(k, parity, at, width):
        size = SLOTS * SLAB_ROWS[k]
        high, low = split(product(dens[k][parity], parity, at, width))
        lanes = pl.ds(parity * FOLD + at, width)
        spec[k][pl.ds(0, size), lanes] = high
        spec[k][pl.ds(size, size), lanes] = low

    def along():
        return sheet[pl.ds(4 * FOLD, 80), pl.ds(0, 240)]

    def along_x(part):
        high, low = split(part)
        return jnp.dot(along(), jnp.concatenate([high, low, high], axis=0), preferred_element_type=F32)

    def middle(j):
        lanes = pl.ds(j * 256, 256)
        table = kernel[:, lanes]
        for q in range(SLOTS // 2):
            def rows_of(shift):
                return [spec[k][pl.ds((shift * SLOTS + 2 * q) * SLAB_ROWS[k], 2 * SLAB_ROWS[k]), lanes] for k in SLABS]

            high, low = rows_of(0), rows_of(1)
            turned = jnp.dot(along(), jnp.concatenate(high + low + high, axis=0), preferred_element_type=F32)
            high, low = split(along_x(turned * table))
            at = 0
            for k in SLABS:
                size = 2 * SLAB_ROWS[k]
                spec[k][pl.ds(q * size, size), lanes] = high[at : at + size]
                spec[k][pl.ds(SLOTS * SLAB_ROWS[k] + q * size, size), lanes] = low[at : at + size]
                at += size

    def backward(k, at, width):
        size = SLAB_ROWS[k]
        even = product(spec[k][:, pl.ds(0, FOLD)], 0, at, width)
        odd = product(spec[k][:, pl.ds(FOLD, FOLD)], 1, at, width)
        near, far = even + odd, even - odd
        if at == MAIN:
            lane = lax.broadcasted_iota(jnp.int32, near.shape, 1)
            near = jnp.where(lane < TAIL, near, pltpu.roll(far, TAIL, 1))
        for p in range(SLOTS):
            mine = slice(p * size, (p + 1) * size)
            if at == MAIN:
                spans = [(WIDE - 128 if size == 16 else MAIN, near[mine])]
                if size < 16:
                    spans = [(MAIN, jnp.concatenate([near[mine], jnp.zeros_like(near[mine])], axis=0))]
            elif size == 16:
                spans = [(at, near[mine]), (MAIN + at, far[mine])]
            else:
                spans = [(at, jnp.concatenate([near[mine], far[mine]], axis=0))]
            for start, value in spans:
                lanes = pl.ds(start, width)
                to_first = value * cols[k][seconds[p], :, lanes].astype(F32)
                to_second = value * rows[k][firsts[p], :, lanes].astype(F32)
                first_sums[k][p, :, lanes] = to_first + first_sums[k][before_first[p], :, lanes]
                second_sums[k][p, :, lanes] = to_second + second_sums[k][before_second[p], :, lanes]

    stored = set()

    def store(k, value):
        if k not in stored:
            stored.add(k)
            kept[k][...] = value
            return
        value = kept[k][...] + value
        size = SLAB_ROWS[k]
        if size == 16:
            near, far, tail = value[:, :MAIN], value[:, MAIN : 2 * MAIN], value[:, 2 * MAIN :]
        else:
            near, far, tail = value[:size, :MAIN], value[size:, :MAIN], value[:size, MAIN:]
        out[pl.ds(16 * k, size), :] = jnp.concatenate([near, tail[:, :TAIL], far, tail[:, TAIL : 2 * TAIL]], axis=1)

    def begin():
        for copy in local:
            copy.start()
        for copy in keeps:
            copy.start()

    def clear():
        for k in SLABS:
            first_sums[k][SLOTS] = jnp.zeros(first_sums[k].shape[1:], F32)
            second_sums[k][SLOTS] = jnp.zeros(second_sums[k].shape[1:], F32)
        for copy in (*local, *keeps):
            copy.wait()
        read_pairs()

    def nothing():
        pass

    tasks, filled = [], []
    for k in SLABS:
        some, messages = gather_tasks(wires, place, k, owns[k], cols[k], rows[k])
        tasks += some
        filled.append(messages)
    tasks.append(Task("begin", [], 0.1, begin))
    tasks.append(Task("clear", ["begin", "z+a10"], 0.5, clear, urgent=False))

    def piece(name, needs, cost, body):
        tasks.append(Task(name, needs, cost, body, urgent=False))

    turned = []
    for k in SLABS:
        weight = SLAB_LANES[k] / WIDE
        for half in range(2):
            piece(f"fill{k}{half}", [*filled[k], "clear"], 0.25 * weight, functools.partial(fill, k, (4 * half, 4 * half + 4)))
        for parity in range(2):
            for at, width in ((0, 512), (512, 384)):
                name = f"forward{k}{parity}{at}"
                turned.append(name)
                piece(name, [f"fill{k}0", f"fill{k}1"], 0.35 * weight, functools.partial(forward, k, parity, at, width))
    def all_middle():
        for j in range(2 * FOLD // 256):
            middle(j)

    piece("middle", turned, 2.5, all_middle)
    for k in SLABS:
        weight = SLAB_LANES[k] / WIDE
        before, names = ["middle"], []
        for at, width in ((0, 256), (256, 256), (512, 256), (768, 128)):
            names.append(f"backward{k}{at}")
            piece(names[-1], before, width / 256 * 0.6 * weight, functools.partial(backward, k, at, width))
        piece(f"backward{k}", names, 0.0, nothing)
        tasks[-1].urgent = True
        tasks += scatter_tasks(
            wires, place, k, functools.partial(last_slot, first_band), functools.partial(last_slot, second_band),
            first_sums[k], second_sums[k], coded[k], codes_in[k], swapped[k], swaps_in[k],
            functools.partial(store, k),
        )
    for task in in_order(tasks)[0]:
        for need in task.needs:
            if need in wires.copies:
                wires.arrive(need)
        task.body()
    for copy in wires.copies.values():
        copy.wait_send()


def exchange(own, pair_list, pair_count):
    vmem = pl.BlockSpec(memory_space=pltpu.VMEM)
    anywhere = pl.BlockSpec(memory_space=pl.ANY)
    sheet, kernel = (jnp.asarray(t) for t in tables())

    def each(shape, kind):
        return [pltpu.VMEM(shape(k), kind) for k in SLABS]

    def stack(count):
        return lambda k: (count, 16, SLAB_LANES[k])

    return pl.pallas_call(
        exchange_kernel,
        out_shape=jax.ShapeDtypeStruct((GX, GX * GX), F32),
        in_specs=[anywhere] * 5,
        out_specs=vmem,
        scratch_shapes=[
            pltpu.VMEM(own.shape, BF16),
            pltpu.SMEM(pair_list.shape, jnp.int32),
            pltpu.SMEM(pair_count.shape, jnp.int32),
            *each(lambda k: (16, SLAB_LANES[k]), BF16),
            *each(stack(BANDS), BF16),
            *each(stack(BANDS), BF16),
            *each(lambda k: (2, 2 * SLOTS * SLAB_ROWS[k], FOLD), BF16),
            *each(lambda k: (2 * SLOTS * SLAB_ROWS[k], 2 * FOLD), BF16),
            *each(stack(SLOTS + 1), F32),
            *each(stack(SLOTS + 1), F32),
            *each(stack(CODED), I16),
            *each(stack(CODED), I16),
            *each(stack(SLOTS), F32),
            *each(stack(SLOTS), F32),
            *each(lambda k: (16, SLAB_LANES[k]), F32),
            pltpu.VMEM(sheet.shape, BF16),
            pltpu.VMEM((80, 2 * FOLD), F32),
            pltpu.SemaphoreType.DMA((COPIES,)),
            pltpu.SemaphoreType.DMA((COPIES,)),
            pltpu.SemaphoreType.DMA((11,)),
        ],
        compiler_params=pltpu.CompilerParams(
            collective_id=0, has_side_effects=True, vmem_limit_bytes=58 * 1024 * 1024
        ),
        name="exchange",
    )(own, pair_list, pair_count, sheet, kernel)


def shards(orbitals, pair_list, pair_count):
    fields = exchange(orbitals.reshape(GX, GX * GX), jnp.swapaxes(pair_list, 1, 2), pair_count)
    return fields.reshape(1, GX * GX * GX)


def solution(mesh):
    return jax.shard_map(
        shards,
        mesh=mesh,
        in_specs=(P(("row", "col"), None), P(("row", "col"), None, None), P(("row", "col"))),
        out_specs=P(("row", "col"), None),
        check_vma=False,
    )
```

```python
import functools

import jax
import jax.numpy as jnp
import ml_dtypes
import numpy as np
from jax import lax
from jax.experimental import pallas as pl
from jax.experimental.pallas import tpu as pltpu
from jax.sharding import PartitionSpec as P

GX = 40
HALF = GX // 2
PART = HALF * GX
MAIN = 768
TAIL = PART - MAIN
WIDE = 2 * MAIN + 128
FOLD = MAIN + 128
SLOTS = 8
BANDS = 16
NZ, NX = 8, 4
SLAB_ROWS = (16, 16, 8)
SLAB_LANES = (WIDE, WIDE, FOLD)
SLABS = range(3)
screen_width = 0.9
MESH = pl.DeviceIdType.MESH
F32, BF16, I16 = jnp.float32, jnp.bfloat16, jnp.int16
TOP = 32767.0
Z_FIRST = (True, False, False)
FAR = (True, False, False)
GATHER_ORDER = (0, 1, 2)
SCATTER_ORDER = (2, 1, 0)
COPIES = 192
CODED = 22
GREETED = ("z+", "z-", "zz+", "zz-", "yh", "x+", "x-", "yl", "core")


def split_np(a):
    high = a.astype(ml_dtypes.bfloat16)
    low = (a - high.astype(np.float64)).astype(ml_dtypes.bfloat16)
    return high, low


@functools.cache
def tables():
    def cas(phase):
        return np.cos(phase) + np.sin(phase)

    n, h = np.arange(GX), np.arange(HALF)
    root = 1.0 / np.sqrt(GX)
    full = cas(2.0 * np.pi * np.outer(n, n) / GX) * root
    even = cas(2.0 * np.pi * np.outer(h, h) / HALF) * root
    odd = cas(2.0 * np.pi * np.outer(2 * h + 1, 2 * h + 1) / (4 * HALF)) * root
    plane = np.zeros((2, FOLD, FOLD))
    plane[0, :PART, :PART] = np.kron(even, full)
    plane[1, :PART, :PART] = np.kron(odd, full)
    plane_high, plane_low = split_np(plane)
    xs = np.concatenate([np.r_[a:b, a:b] for a, b in ((0, 16), (16, 32), (32, 40))])
    pair = np.concatenate([np.r_[[0] * k, [1] * k] for k in (16, 16, 8)])
    both = np.where(pair[:, None] == pair[None, :], full[xs][:, xs], 0.0)
    high, low = split_np(both)
    along = np.concatenate([high, high, low], axis=1)
    signed = np.where(n < GX // 2, n, n - GX) * (2.0 * np.pi / GX)
    squared = signed**2
    total = squared[:, None, None] + squared[None, :, None] + squared[None, None, :]
    safe = np.where(total > 0, total, 1.0)
    screened = 4.0 * np.pi * (1.0 - np.exp(-safe / (4.0 * screen_width**2))) / safe
    kernel = np.where(total > 0, screened, np.pi / screen_width**2)
    padded = np.zeros((GX, 2, FOLD), np.float32)
    padded[:, 0, :PART] = kernel[:, 0::2].reshape(GX, PART)
    padded[:, 1, :PART] = kernel[:, 1::2].reshape(GX, PART)
    sheet = np.zeros((4 * FOLD + 80, FOLD), ml_dtypes.bfloat16)
    sheet[: 2 * FOLD] = plane_high.reshape(2 * FOLD, FOLD)
    sheet[2 * FOLD : 4 * FOLD] = plane_low.reshape(2 * FOLD, FOLD)
    sheet[4 * FOLD :, :240] = along
    return sheet, np.tile(padded.reshape(GX, 2 * FOLD)[xs], (12, 1))


def split(x):
    high = x.astype(BF16)
    return high, (x - high.astype(F32)).astype(BF16)


def encode(value):
    most = jnp.max(jnp.abs(value), axis=1, keepdims=True)
    power = jnp.floor(jnp.log(jnp.maximum(most, 1e-30)) * 1.4426950408889634)
    share = value * (0.5 * jnp.exp2(-power))
    root = share * lax.rsqrt(jnp.maximum(jnp.abs(share), 1e-20))
    code = jnp.clip(jnp.round(root * TOP), -TOP, TOP)
    lanes = lax.broadcasted_iota(jnp.int32, (value.shape[0], 128), 1)
    last = jnp.where(lanes >= 64, power, code[:, -128:])
    return jnp.concatenate([code[:, :-128], last], axis=1).astype(jnp.int32).astype(I16)


def decode(code):
    wide = code.astype(jnp.int32).astype(F32)
    scale = jnp.exp2(wide[:, -64:-63]) * (2.0 / (TOP * TOP))
    return wide * jnp.abs(wide) * scale


def places():
    r, c = lax.axis_index("row"), lax.axis_index("col")
    z, yh = r // 2, r % 2
    x, yl, core = c // 4, (c // 2) % 2, c % 2

    def row_of(dz, y):
        return ((z + dz + NZ) % NZ) * 2 + y

    def col_of(dx, y, k):
        return ((x + dx + NX) % NX) * 4 + y * 2 + k

    ids = {
        "z+": (row_of(1, yh), c),
        "z-": (row_of(-1, yh), c),
        "zf": (row_of(1 - 2 * core, yh), c),
        "zg": (row_of(2 * core - 1, yh), c),
        "zz+": (row_of(2, yh), c),
        "zz-": (row_of(-2, yh), c),
        "zzf": (row_of(2 - 4 * core, yh), c),
        "yh": (row_of(0, 1 - yh), c),
        "x+": (r, col_of(1, yl, core)),
        "x-": (r, col_of(-1, yl, core)),
        "yl": (r, col_of(0, 1 - yl, core)),
        "core": (r, col_of(0, yl, 1 - core)),
    }
    return r, c, yh, yl, core, row_of, col_of, ids


def place_sign(core):
    return 1 - 2 * core


def greet(ids):
    barrier = pltpu.get_barrier_semaphore()
    for where in GREETED:
        pl.semaphore_signal(barrier, inc=1, device_id=ids[where], device_id_type=MESH)


def met():
    pl.semaphore_wait(pltpu.get_barrier_semaphore(), len(GREETED))


class Wires:
    def __init__(self, send_sem, recv_sem, ids):
        self.send_sem, self.recv_sem, self.ids = send_sem, recv_sem, ids
        self.copies, self.waited = {}, set()

    def start(self, name, source, target, where):
        at = len(self.copies)
        copy = pltpu.make_async_remote_copy(
            src_ref=source,
            dst_ref=target,
            send_sem=self.send_sem.at[at],
            recv_sem=self.recv_sem.at[at],
            device_id=self.ids[where],
            device_id_type=MESH,
        )
        copy.start()
        self.copies[name] = copy

    def arrive(self, name):
        if name not in self.waited:
            self.waited.add(name)
            self.copies[name].wait_recv()


RATES = {"z": 1 / 49e3, "x": 1 / 49e3, "y": 1 / 49e3, "l": 1 / 49e3, "c": 1 / 400e3}
DELAYS = {"z": 2.9, "x": 2.9, "y": 3.2, "l": 2.9, "c": 0.7}


class Task:
    def __init__(self, name, needs, cost, body, emits=(), rank=0):
        self.name, self.needs, self.cost, self.body = name, list(needs), cost, body
        self.emits, self.rank = list(emits), rank


def in_order(tasks):
    known, free, left, order, now = {}, {}, list(tasks), [], 0.0
    while left:
        ready = []
        for i, task in enumerate(left):
            if all(need in known for need in task.needs):
                at = max([known[need] for need in task.needs], default=0.0)
                ready.append((max(at, now), task.rank, at, i))
        at, _, _, i = min(ready)
        task = left.pop(i)
        now = at + task.cost
        known[task.name] = now
        for message, (link, hops), size in task.emits:
            time = size * RATES[link[0]]
            begin = max(now, free.get(link, 0.0))
            free[link] = begin + time * hops
            known[message] = begin + time + DELAYS[link[0]] + 1.0 * (hops - 1)
        task.needs.sort(key=known.get)
        order.append(task)
    return order, now


LINKS = {
    "z+": ("z+", 1), "z-": ("z-", 1), "zf": ("z+", 1), "zg": ("z-", 1), "zz+": ("z+", 2), "zz-": ("z-", 2), "zzf": ("z+", 2),
    "x+": ("x+", 1), "x-": ("x-", 1), "yh": ("y", 1), "yl": ("l", 1), "core": ("c", 1),
}


def gather_tasks(wires, place, k, own, cols, rows):
    r, c, yh, yl, core, row_of, col_of, _ = place
    size = 16 * SLAB_LANES[k] * 2
    tasks = []
    messages = []

    def task(name, needs, sends):
        def body():
            for message, where, block, index, source in sends:
                target = block.at[index]
                wires.start(f"{message}{k}", target if source is None else source, target, where)

        emits = [(f"{send[0]}{k}", LINKS[send[1]], size) for send in sends]
        messages.extend(send[0] for send in sends)
        tasks.append(Task(f"gather {name}{k}", [f"{need}{k}" for need in needs], 0.03 * len(sends), body, emits))

    x_first = [("x+a0", "x+", rows, c, own), ("x-a0", "x-", rows, c, own), ("yl", "yl", rows, c, own), ("k0", "core", rows, c, own)]
    if Z_FIRST[k]:
        sign = place_sign(core)
        task("own", [], [("fa0", "zf", cols, r, own), ("ga0", "zg", cols, r, own), ("y0", "yh", cols, r, own), *x_first])
        for way, turn in (("f", -1), ("g", 1)):
            for step in range(3):
                index = row_of(turn * sign * (step + 1), yh)
                sends = [(f"{way}a{step + 1}", "z" + way, cols, index, None)] if step < 2 else []
                if way == "f" and step == (1 if FAR[k] else 2):
                    sends.append(("fa3", "zzf" if FAR[k] else "zf", cols, index, None))
                task(f"{way}{step}", [f"{way}a{step}"], [*sends, (f"y{way}{step}", "yh", cols, index, None)])
        task("far", ["fa3"], [("yf3", "yh", cols, row_of(4, yh), None)])
    else:
        beside = [("z+a0", "z+", cols, r, own), ("z-a0", "z-", cols, r, own)]
        task("own", [], [*beside, ("y0", "yh", cols, r, own), *x_first])
        other = row_of(0, 1 - yh)
        task("y", ["y0"], [("z+b0", "z+", cols, other, None), ("z-b0", "z-", cols, other, None)])
        for where, turn, long in (("z+", -1, "a"), ("z-", 1, "b")):
            for which, y in (("a", yh), ("b", 1 - yh)):
                for step in range(3 if which == long and not FAR[k] else 2):
                    index = row_of(turn * (step + 1), y)
                    sends = [(f"{where}{which}{step + 1}", where, cols, index, None)]
                    if which == long and FAR[k] and step == 1:
                        sends.append((f"{where}{which}3", "z" + where, cols, index, None))
                    task(f"{where}{which}{step}", [f"{where}{which}{step}"], sends)
    other = col_of(0, 1 - yl, core)
    task("l", ["yl"], [("x+b0", "x+", rows, other, None), ("x-b0", "x-", rows, other, None), ("k1", "core", rows, other, None)])
    for where, turn, long in (("x+", -1, "a"), ("x-", 1, "b")):
        for which, y in (("a", yl), ("b", 1 - yl)):
            index = col_of(turn, y, core)
            sends = [(f"{where}{which}1", where, rows, index, None)] if which == long else []
            task(f"{where}{which}", [f"{where}{which}0"], [*sends, (f"k{where}{which}0", "core", rows, index, None)])
        index = col_of(2, yl if long == "a" else 1 - yl, core)
        task(f"{where}far", [f"{where}{long}1"], [(f"k{where}far", "core", rows, index, None)])
    return tasks, [f"{message}{k}" for message in messages]


def scatter_tasks(wires, place, k, first_at, second_at, firsts, seconds, coded, codes_in, swapped, swaps_in, store):
    r, c, yh, yl, core, row_of, col_of, _ = place
    size = 16 * SLAB_LANES[k] * 2
    weight = SLAB_LANES[k] / WIDE
    tasks, slots = [], {}

    def term(index):
        return seconds[second_at(index)]

    def arrived(message):
        return decode(codes_in[slots[message]])

    def total(value, needs):
        for need in needs:
            value = value + arrived(need)
        return value

    def send(message, where, value, needs, after=(), rank=0):
        slots[message] = len(slots)

        def body():
            slot = slots[message]
            coded[slot] = encode(total(value(), needs))
            wires.start(f"{message}/{k}", coded.at[slot], codes_in.at[slot], where)

        needed = [f"{need}/{k}" for need in (*needs, *after)] + [f"backward{k}"]
        cost = 0.03 + weight * (0.08 + 0.02 * len(needs))
        tasks.append(Task(f"scatter {message}{k}", needed, cost, body, [(f"{message}/{k}", LINKS[where], size)], rank))

    def keep(name, value, needs, after=()):
        def body():
            store(total(value(), needs))

        needed = [f"{need}/{k}" for need in (*needs, *after)] + [f"backward{k}"]
        tasks.append(Task(f"keep {name}{k}", needed, 0.04 * weight, body, rank=2))

    def of(index):
        return functools.partial(term, index)

    order = [(2, "a"), (2, "b"), (1, "b"), (-1, "a"), (1, "a"), (-1, "b"), (0, "b"), (0, "a")]
    y_of = {"a": yl, "b": 1 - yl}

    def swap_all(some):
        def body():
            for slot in some:
                dx, y = order[slot]
                swapped[slot] = firsts[first_at(col_of(dx, y_of[y], 1 - core))]
                wires.start(f"swap{dx}{y}/{k}", swapped.at[slot], swaps_in.at[slot], "core")

        emits = [(f"swap{order[slot][0]}{order[slot][1]}/{k}", LINKS["core"], 2 * size) for slot in some]
        tasks.append(Task(f"swap{some[0]}{k}", [f"backward{k}"], 0.04 * len(some), body, emits, rank=2))

    def chip_sum(dx, y):
        return firsts[first_at(col_of(dx, y_of[y], core))] + swaps_in[order.index((dx, y))]

    def of_chip(dx, y):
        return functools.partial(chip_sum, dx, y)

    if Z_FIRST[k]:
        sign = place_sign(core)
        spots = {"f3": 4, "f2": 3 * sign, "g2": -3 * sign, "f1": 2 * sign, "g1": -2 * sign, "f0": sign, "g0": -sign, "0": 0}
        for i, (spot, dz) in enumerate(spots.items()):
            send(f"y{spot}", "yh", of(row_of(dz, 1 - yh)), ())
            if i == 1:
                swap_all(range(0, 4))
            if i == 3:
                swap_all(range(4, 8))
        before = {"f3": (), "f2": () if FAR[k] else ("pf3",), "g2": (), "f1": ("pf2", "pf3") if FAR[k] else ("pf2",)}
        before |= {"g1": ("pg2",), "f0": ("pf1",), "g0": ("pg1",)}
        for spot, needs in before.items():
            where = "zzf" if FAR[k] and spot == "f3" else "z" + spot[0]
            send(f"p{spot}", where, of(row_of(spots[spot], yh)), (f"y{spot}", *needs))
        keep("z", of(row_of(0, yh)), ("y0", "pf0", "pg0"))
    else:
        y_row = {"a": yh, "b": 1 - yh}

        def chain(where, turn, which, distance, needs):
            way = "z" + where if FAR[k] and distance == 4 else where
            send(f"p{where}{which}{distance}", way, of(row_of(turn * distance, y_row[which])), needs)

        chain("z+", 1, "a", 4, ())
        chain("z-", -1, "b", 4, ())
        swap_all(range(0, 4))
        chain("z+", 1, "b", 3, ())
        chain("z-", -1, "a", 3, ())
        swap_all(range(4, 8))
        for where, turn, long in (("z+", 1, "a"), ("z-", -1, "b")):
            for which in "ab":
                for distance in range(3 if which == long else 2, 0, -1):
                    needs = [f"p{where}{which}{distance + 1}"]
                    if which == long and FAR[k]:
                        needs = [] if distance == 3 else [*needs, f"p{where}{which}4"] if distance == 2 else needs
                    chain(where, turn, which, distance, needs)
        send("yb", "yh", of(row_of(0, 1 - yh)), ("pz+b1", "pz-b1"))
        keep("z", of(row_of(0, yh)), ("pz+a1", "pz-a1", "yb"))
    send("qx+a2", "x+", of_chip(2, "a"), (), ("swap2a",), 2)
    send("qx-b2", "x-", of_chip(2, "b"), (), ("swap2b",), 2)
    send("qx+b1", "x+", of_chip(1, "b"), (), ("swap1b",), 2)
    send("qx-a1", "x-", of_chip(-1, "a"), (), ("swap-1a",), 2)
    send("qx+a1", "x+", of_chip(1, "a"), ("qx+a2",), ("swap1a",), 2)
    send("qx-b1", "x-", of_chip(-1, "b"), ("qx-b2",), ("swap-1b",), 2)
    send("lb", "yl", of_chip(0, "b"), ("qx+b1", "qx-b1"), ("swap0b",), 2)
    keep("x", of_chip(0, "a"), ("qx+a1", "qx-a1", "lb"), ("swap0a",))
    return tasks


def fold(rho, slab):
    rows = SLAB_ROWS[slab]
    if rows == 16:
        near, far, tail = rho[:, :MAIN], rho[:, MAIN : 2 * MAIN], rho[:, 2 * MAIN :]
    else:
        near, far, tail = rho[:rows, :MAIN], rho[rows:, :MAIN], rho[:rows, MAIN:]
    moved = pltpu.roll(tail, 128 - TAIL, 1)
    even = jnp.concatenate([near + far, tail + moved], axis=1)
    return even, jnp.concatenate([near - far, tail - moved], axis=1)


def exchange_kernel(
    own_in, pair_list_in, pair_count_in, sheet_in, kernel_in, out,
    own, pair_list, pair_count, own_0, own_1, own_2, cols_0, cols_1, cols_2, rows_0, rows_1, rows_2,
    dens_0, dens_1, dens_2, spec_0, spec_1, spec_2, first_0, first_1, first_2,
    second_0, second_1, second_2, coded_0, coded_1, coded_2, codes_in_0, codes_in_1, codes_in_2,
    swapped_0, swapped_1, swapped_2, swaps_in_0, swaps_in_1, swaps_in_2,
    kept_0, kept_1, kept_2, sheet, kernel, send_sem, recv_sem, local_sem,
):
    owns, cols, rows = (own_0, own_1, own_2), (cols_0, cols_1, cols_2), (rows_0, rows_1, rows_2)
    dens, spec = (dens_0, dens_1, dens_2), (spec_0, spec_1, spec_2)
    first_sums, second_sums = (first_0, first_1, first_2), (second_0, second_1, second_2)
    coded, codes_in = (coded_0, coded_1, coded_2), (codes_in_0, codes_in_1, codes_in_2)
    kept = (kept_0, kept_1, kept_2)
    swapped, swaps_in = (swapped_0, swapped_1, swapped_2), (swaps_in_0, swaps_in_1, swaps_in_2)
    place = places()
    r, c, ids = place[0], place[1], place[-1]

    local = [
        pltpu.make_async_copy(sheet_in, sheet, local_sem.at[0]),
        pltpu.make_async_copy(kernel_in.at[pl.ds(0, 80)], kernel, local_sem.at[1]),
        pltpu.make_async_copy(pair_list_in, pair_list, local_sem.at[2]),
        pltpu.make_async_copy(pair_count_in, pair_count, local_sem.at[3]),
    ]
    greet(ids)
    take = pltpu.make_async_copy(own_in, own, local_sem.at[10])
    take.start()
    take.wait()
    for k in SLABS:
        size = SLAB_ROWS[k]
        band = own[pl.ds(16 * k, size), :].astype(F32)
        tails = [band[:, MAIN:PART], band[:, PART + MAIN :], jnp.zeros((size, 128 - 2 * TAIL), F32)]
        near, far, tail = band[:, :MAIN], band[:, PART : PART + MAIN], jnp.concatenate(tails, axis=1)
        if size == 16:
            owns[k][...] = jnp.concatenate([near, far, tail], axis=1).astype(BF16)
        else:
            low_rows = jnp.concatenate([far, jnp.zeros((size, 128), F32)], axis=1)
            owns[k][...] = jnp.concatenate([jnp.concatenate([near, tail], axis=1), low_rows], axis=0).astype(BF16)
    met()
    wires = Wires(send_sem, recv_sem, ids)
    keeps = []
    for k in SLABS:
        keeps.append(pltpu.make_async_copy(owns[k], cols[k].at[r], local_sem.at[4 + 2 * k]))
        keeps.append(pltpu.make_async_copy(owns[k], rows[k].at[c], local_sem.at[5 + 2 * k]))

    firsts, seconds, first_band, second_band, before_first, before_second = [], [], [], [], [], []

    def last_slot(bands, wanted):
        at = SLOTS
        for p, band in enumerate(bands):
            at = jnp.where(band == wanted, p, at)
        return at

    def read_pairs():
        count = pair_count[0]
        for p in range(SLOTS):
            first, second = pair_list[0, 0, p], pair_list[0, 1, p]
            other = r * BANDS + first != second * BANDS + c
            firsts.append(first)
            seconds.append(second)
            first_band.append(jnp.where(p < count, first, -1))
            second_band.append(jnp.where((p < count) & other, second, -1))
            before_first.append(last_slot(first_band[:p], first_band[p]))
            before_second.append(last_slot(second_band[:p], second_band[p]))

    def density(k, p):
        return rows[k][firsts[p]].astype(F32) * cols[k][seconds[p]].astype(F32)

    def fill(k, slots):
        size = SLAB_ROWS[k]
        group = 16 // size
        for p in range(slots[0], slots[1], group):
            parts = [fold(density(k, p + i), k) for i in range(group)]
            for parity in range(2):
                value = jnp.concatenate([part[parity] for part in parts], axis=0)
                high, low = split(value)
                dens[k][parity, pl.ds(p * size, 16), :] = high
                dens[k][parity, pl.ds((SLOTS + p) * size, 16), :] = low

    def product(values, parity, at, width):
        lanes = pl.ds(at, width)
        half = values.shape[0] // 2
        wide = jnp.dot(values, sheet[pl.ds(parity * FOLD, FOLD), lanes], preferred_element_type=F32)
        thin = jnp.dot(values[:half], sheet[pl.ds((2 + parity) * FOLD, FOLD), lanes], preferred_element_type=F32)
        return wide[:half] + wide[half:] + thin

    def forward(k, parity, at, width):
        size = SLOTS * SLAB_ROWS[k]
        high, low = split(product(dens[k][parity], parity, at, width))
        lanes = pl.ds(parity * FOLD + at, width)
        spec[k][pl.ds(0, size), lanes] = high
        spec[k][pl.ds(size, size), lanes] = low

    def along():
        return sheet[pl.ds(4 * FOLD, 80), pl.ds(0, 240)]

    def along_x(part):
        high, low = split(part)
        return jnp.dot(along(), jnp.concatenate([high, low, high], axis=0), preferred_element_type=F32)

    def middle(j):
        lanes = pl.ds(j * 256, 256)
        table = kernel[:, lanes]
        for q in range(SLOTS // 2):
            def rows_of(shift):
                return [spec[k][pl.ds((shift * SLOTS + 2 * q) * SLAB_ROWS[k], 2 * SLAB_ROWS[k]), lanes] for k in SLABS]

            high, low = rows_of(0), rows_of(1)
            turned = jnp.dot(along(), jnp.concatenate(high + low + high, axis=0), preferred_element_type=F32)
            high, low = split(along_x(turned * table))
            at = 0
            for k in SLABS:
                size = 2 * SLAB_ROWS[k]
                spec[k][pl.ds(q * size, size), lanes] = high[at : at + size]
                spec[k][pl.ds(SLOTS * SLAB_ROWS[k] + q * size, size), lanes] = low[at : at + size]
                at += size

    def backward(k, at, width):
        size = SLAB_ROWS[k]
        even = product(spec[k][:, pl.ds(0, FOLD)], 0, at, width)
        odd = product(spec[k][:, pl.ds(FOLD, FOLD)], 1, at, width)
        near, far = even + odd, even - odd
        if at == MAIN:
            lane = lax.broadcasted_iota(jnp.int32, near.shape, 1)
            near = jnp.where(lane < TAIL, near, pltpu.roll(far, TAIL, 1))
        for p in range(SLOTS):
            mine = slice(p * size, (p + 1) * size)
            if at == MAIN:
                spans = [(WIDE - 128 if size == 16 else MAIN, near[mine])]
                if size < 16:
                    spans = [(MAIN, jnp.concatenate([near[mine], jnp.zeros_like(near[mine])], axis=0))]
            elif size == 16:
                spans = [(at, near[mine]), (MAIN + at, far[mine])]
            else:
                spans = [(at, jnp.concatenate([near[mine], far[mine]], axis=0))]
            for start, value in spans:
                lanes = pl.ds(start, width)
                to_first = value * cols[k][seconds[p], :, lanes].astype(F32)
                to_second = value * rows[k][firsts[p], :, lanes].astype(F32)
                first_sums[k][p, :, lanes] = to_first + first_sums[k][before_first[p], :, lanes]
                second_sums[k][p, :, lanes] = to_second + second_sums[k][before_second[p], :, lanes]

    stored = set()

    def store(k, value):
        if k not in stored:
            stored.add(k)
            kept[k][...] = value
            return
        value = kept[k][...] + value
        size = SLAB_ROWS[k]
        if size == 16:
            near, far, tail = value[:, :MAIN], value[:, MAIN : 2 * MAIN], value[:, 2 * MAIN :]
        else:
            near, far, tail = value[:size, :MAIN], value[size:, :MAIN], value[:size, MAIN:]
        out[pl.ds(16 * k, size), :] = jnp.concatenate([near, tail[:, :TAIL], far, tail[:, TAIL : 2 * TAIL]], axis=1)

    def begin():
        for copy in local:
            copy.start()
        for copy in keeps:
            copy.start()

    def clear():
        for k in SLABS:
            first_sums[k][SLOTS] = jnp.zeros(first_sums[k].shape[1:], F32)
            second_sums[k][SLOTS] = jnp.zeros(second_sums[k].shape[1:], F32)
        for copy in (*local, *keeps):
            copy.wait()
        read_pairs()

    def nothing():
        pass

    tasks, filled = [], {}
    for k in GATHER_ORDER:
        some, messages = gather_tasks(wires, place, k, owns[k], cols[k], rows[k])
        tasks += some
        filled[k] = messages
    tasks.append(Task("begin", [], 0.1, begin))
    tasks.append(Task("clear", ["begin", "fa10" if Z_FIRST[0] else "z+a10"], 0.5, clear, rank=1))

    def piece(name, needs, cost, body):
        tasks.append(Task(name, needs, cost, body, rank=1))

    turned = []
    for k in GATHER_ORDER:
        weight = SLAB_LANES[k] / WIDE
        for half in range(2):
            piece(f"fill{k}{half}", [*filled[k], "clear"], 0.25 * weight, functools.partial(fill, k, (4 * half, 4 * half + 4)))
        for parity in range(2):
            for at, width in ((0, 512), (512, 384)):
                name = f"forward{k}{parity}{at}"
                turned.append(name)
                piece(name, [f"fill{k}0", f"fill{k}1"], 0.3 * weight, functools.partial(forward, k, parity, at, width))
    def all_middle():
        for j in range(2 * FOLD // 256):
            middle(j)

    piece("middle", turned, 2.5, all_middle)
    for k in SCATTER_ORDER:
        weight = SLAB_LANES[k] / WIDE
        before, names = ["middle"], []
        for at, width in ((0, 256), (256, 256), (512, 256), (768, 128)):
            names.append(f"backward{k}{at}")
            piece(names[-1], before, width / 256 * 0.6 * weight, functools.partial(backward, k, at, width))
        piece(f"backward{k}", names, 0.0, nothing)
        tasks[-1].rank = 0
        tasks += scatter_tasks(
            wires, place, k, functools.partial(last_slot, first_band), functools.partial(last_slot, second_band),
            first_sums[k], second_sums[k], coded[k], codes_in[k], swapped[k], swaps_in[k],
            functools.partial(store, k),
        )
    for task in in_order(tasks)[0]:
        for need in task.needs:
            if need in wires.copies:
                wires.arrive(need)
        task.body()
    for copy in wires.copies.values():
        copy.wait_send()


def exchange(own, pair_list, pair_count):
    vmem = pl.BlockSpec(memory_space=pltpu.VMEM)
    anywhere = pl.BlockSpec(memory_space=pl.ANY)
    sheet, kernel = (jnp.asarray(t) for t in tables())

    def each(shape, kind):
        return [pltpu.VMEM(shape(k), kind) for k in SLABS]

    def stack(count):
        return lambda k: (count, 16, SLAB_LANES[k])

    return pl.pallas_call(
        exchange_kernel,
        out_shape=jax.ShapeDtypeStruct((GX, GX * GX), F32),
        in_specs=[anywhere] * 5,
        out_specs=vmem,
        scratch_shapes=[
            pltpu.VMEM(own.shape, BF16),
            pltpu.SMEM(pair_list.shape, jnp.int32),
            pltpu.SMEM(pair_count.shape, jnp.int32),
            *each(lambda k: (16, SLAB_LANES[k]), BF16),
            *each(stack(BANDS), BF16),
            *each(stack(BANDS), BF16),
            *each(lambda k: (2, 2 * SLOTS * SLAB_ROWS[k], FOLD), BF16),
            *each(lambda k: (2 * SLOTS * SLAB_ROWS[k], 2 * FOLD), BF16),
            *each(stack(SLOTS + 1), F32),
            *each(stack(SLOTS + 1), F32),
            *each(stack(CODED), I16),
            *each(stack(CODED), I16),
            *each(stack(SLOTS), F32),
            *each(stack(SLOTS), F32),
            *each(lambda k: (16, SLAB_LANES[k]), F32),
            pltpu.VMEM(sheet.shape, BF16),
            pltpu.VMEM((80, 2 * FOLD), F32),
            pltpu.SemaphoreType.DMA((COPIES,)),
            pltpu.SemaphoreType.DMA((COPIES,)),
            pltpu.SemaphoreType.DMA((11,)),
        ],
        compiler_params=pltpu.CompilerParams(
            collective_id=0, has_side_effects=True, vmem_limit_bytes=58 * 1024 * 1024
        ),
        name="exchange",
    )(own, pair_list, pair_count, sheet, kernel)


def shards(orbitals, pair_list, pair_count):
    fields = exchange(orbitals.reshape(GX, GX * GX), jnp.swapaxes(pair_list, 1, 2), pair_count)
    return fields.reshape(1, GX * GX * GX)


def solution(mesh):
    return jax.shard_map(
        shards,
        mesh=mesh,
        in_specs=(P(("row", "col"), None), P(("row", "col"), None, None), P(("row", "col"))),
        out_specs=P(("row", "col"), None),
        check_vma=False,
    )
```

```python
import functools

import jax
import jax.numpy as jnp
import ml_dtypes
import numpy as np
from jax import lax
from jax.experimental import pallas as pl
from jax.experimental.pallas import tpu as pltpu
from jax.sharding import PartitionSpec as P

GX = 40
HALF = GX // 2
PART = HALF * GX
MAIN = 768
TAIL = PART - MAIN
WIDE = 2 * MAIN + 128
FOLD = MAIN + 128
SLOTS = 8
BANDS = 16
NZ, NX = 8, 4
SLAB_ROWS = (16, 16, 8)
SLAB_LANES = (WIDE, WIDE, FOLD)
SLABS = range(3)
screen_width = 0.9
MESH = pl.DeviceIdType.MESH
F32, BF16, I16 = jnp.float32, jnp.bfloat16, jnp.int16
TOP = 32767.0
Z_FIRST = (True, False, False)
FAR = (True, False, False)
GATHER_ORDER = (2, 0, 1)
SCATTER_ORDER = (1, 2, 0)
COPIES = 192
CODED = 22
GREETED = ("z+", "z-", "zz+", "zz-", "yh", "x+", "x-", "yl", "core")


def split_np(a):
    high = a.astype(ml_dtypes.bfloat16)
    low = (a - high.astype(np.float64)).astype(ml_dtypes.bfloat16)
    return high, low


@functools.cache
def tables():
    def cas(phase):
        return np.cos(phase) + np.sin(phase)

    n, h = np.arange(GX), np.arange(HALF)
    root = 1.0 / np.sqrt(GX)
    full = cas(2.0 * np.pi * np.outer(n, n) / GX) * root
    even = cas(2.0 * np.pi * np.outer(h, h) / HALF) * root
    odd = cas(2.0 * np.pi * np.outer(2 * h + 1, 2 * h + 1) / (4 * HALF)) * root
    plane = np.zeros((2, FOLD, FOLD))
    plane[0, :PART, :PART] = np.kron(even, full)
    plane[1, :PART, :PART] = np.kron(odd, full)
    plane_high, plane_low = split_np(plane)
    xs = np.concatenate([np.r_[a:b, a:b] for a, b in ((0, 16), (16, 32), (32, 40))])
    pair = np.concatenate([np.r_[[0] * k, [1] * k] for k in (16, 16, 8)])
    both = np.where(pair[:, None] == pair[None, :], full[xs][:, xs], 0.0)
    high, low = split_np(both)
    along = np.concatenate([high, high, low], axis=1)
    signed = np.where(n < GX // 2, n, n - GX) * (2.0 * np.pi / GX)
    squared = signed**2
    total = squared[:, None, None] + squared[None, :, None] + squared[None, None, :]
    safe = np.where(total > 0, total, 1.0)
    screened = 4.0 * np.pi * (1.0 - np.exp(-safe / (4.0 * screen_width**2))) / safe
    kernel = np.where(total > 0, screened, np.pi / screen_width**2)
    padded = np.zeros((GX, 2, FOLD), np.float32)
    padded[:, 0, :PART] = kernel[:, 0::2].reshape(GX, PART)
    padded[:, 1, :PART] = kernel[:, 1::2].reshape(GX, PART)
    sheet = np.zeros((4 * FOLD + 80, FOLD), ml_dtypes.bfloat16)
    sheet[: 2 * FOLD] = plane_high.reshape(2 * FOLD, FOLD)
    sheet[2 * FOLD : 4 * FOLD] = plane_low.reshape(2 * FOLD, FOLD)
    sheet[4 * FOLD :, :240] = along
    return sheet, padded.reshape(GX, 2 * FOLD)[xs]


def split(x):
    high = x.astype(BF16)
    return high, (x - high.astype(F32)).astype(BF16)


def encode(value):
    most = jnp.max(jnp.abs(value), axis=1, keepdims=True)
    power = jnp.floor(jnp.log(jnp.maximum(most, 1e-30)) * 1.4426950408889634)
    share = value * (0.5 * jnp.exp2(-power))
    root = share * lax.rsqrt(jnp.maximum(jnp.abs(share), 1e-20))
    code = jnp.clip(jnp.round(root * TOP), -TOP, TOP)
    lanes = lax.broadcasted_iota(jnp.int32, (value.shape[0], 128), 1)
    last = jnp.where(lanes >= 64, power, code[:, -128:])
    return jnp.concatenate([code[:, :-128], last], axis=1).astype(jnp.int32).astype(I16)


def decode(code):
    wide = code.astype(jnp.int32).astype(F32)
    scale = jnp.exp2(wide[:, -64:-63]) * (2.0 / (TOP * TOP))
    return wide * jnp.abs(wide) * scale


def places():
    r, c = lax.axis_index("row"), lax.axis_index("col")
    z, yh = r // 2, r % 2
    x, yl, core = c // 4, (c // 2) % 2, c % 2

    def row_of(dz, y):
        return ((z + dz + NZ) % NZ) * 2 + y

    def col_of(dx, y, k):
        return ((x + dx + NX) % NX) * 4 + y * 2 + k

    ids = {
        "z+": (row_of(1, yh), c),
        "z-": (row_of(-1, yh), c),
        "zf": (row_of(1 - 2 * core, yh), c),
        "zg": (row_of(2 * core - 1, yh), c),
        "zz+": (row_of(2, yh), c),
        "zz-": (row_of(-2, yh), c),
        "zzf": (row_of(2 - 4 * core, yh), c),
        "yh": (row_of(0, 1 - yh), c),
        "x+": (r, col_of(1, yl, core)),
        "x-": (r, col_of(-1, yl, core)),
        "yl": (r, col_of(0, 1 - yl, core)),
        "core": (r, col_of(0, yl, 1 - core)),
    }
    return r, c, yh, yl, core, row_of, col_of, ids


def place_sign(core):
    return 1 - 2 * core


def greet(ids):
    barrier = pltpu.get_barrier_semaphore()
    for where in GREETED:
        pl.semaphore_signal(barrier, inc=1, device_id=ids[where], device_id_type=MESH)


def met():
    pl.semaphore_wait(pltpu.get_barrier_semaphore(), len(GREETED))


class Wires:
    def __init__(self, send_sem, recv_sem, ids):
        self.send_sem, self.recv_sem, self.ids = send_sem, recv_sem, ids
        self.copies, self.waited = {}, set()

    def start(self, name, source, target, where):
        at = len(self.copies)
        copy = pltpu.make_async_remote_copy(
            src_ref=source,
            dst_ref=target,
            send_sem=self.send_sem.at[at],
            recv_sem=self.recv_sem.at[at],
            device_id=self.ids[where],
            device_id_type=MESH,
        )
        copy.start()
        self.copies[name] = copy

    def arrive(self, name):
        if name not in self.waited:
            self.waited.add(name)
            self.copies[name].wait_recv()


RATES = {"z": 1 / 49e3, "x": 1 / 49e3, "y": 1 / 49e3, "l": 1 / 49e3, "c": 1 / 400e3}
DELAYS = {"z": 2.9, "x": 2.9, "y": 3.2, "l": 2.9, "c": 0.7}


class Task:
    def __init__(self, name, needs, cost, body, emits=(), rank=0):
        self.name, self.needs, self.cost, self.body = name, list(needs), cost, body
        self.emits, self.rank = list(emits), rank


def in_order(tasks):
    known, free, left, order, now = {}, {}, list(tasks), [], 0.0
    while left:
        ready = []
        for i, task in enumerate(left):
            if all(need in known for need in task.needs):
                at = max([known[need] for need in task.needs], default=0.0)
                ready.append((max(at, now), task.rank, at, i))
        at, _, _, i = min(ready)
        task = left.pop(i)
        now = at + task.cost
        known[task.name] = now
        for message, (link, hops), size in task.emits:
            time = size * RATES[link[0]]
            begin = max(now, free.get(link, 0.0))
            free[link] = begin + time * hops
            known[message] = begin + time + DELAYS[link[0]] + 1.0 * (hops - 1)
        task.needs.sort(key=known.get)
        order.append(task)
    return order, now


LINKS = {
    "z+": ("z+", 1), "z-": ("z-", 1), "zf": ("z+", 1), "zg": ("z-", 1), "zz+": ("z+", 2), "zz-": ("z-", 2), "zzf": ("z+", 2),
    "x+": ("x+", 1), "x-": ("x-", 1), "yh": ("y", 1), "yl": ("l", 1), "core": ("c", 1),
}


def gather_tasks(wires, place, k, own, cols, rows):
    r, c, yh, yl, core, row_of, col_of, _ = place
    size = 16 * SLAB_LANES[k] * 2
    tasks = []
    messages = []

    def task(name, needs, sends):
        def body():
            for message, where, block, index, source in sends:
                target = block.at[index]
                wires.start(f"{message}{k}", target if source is None else source, target, where)

        emits = [(f"{send[0]}{k}", LINKS[send[1]], size) for send in sends]
        messages.extend(send[0] for send in sends)
        tasks.append(Task(f"gather {name}{k}", [f"{need}{k}" for need in needs], 0.03 * len(sends), body, emits))

    x_first = [("x+a0", "x+", rows, c, own), ("x-a0", "x-", rows, c, own), ("yl", "yl", rows, c, own), ("k0", "core", rows, c, own)]
    if Z_FIRST[k]:
        sign = place_sign(core)
        task("own", [], [("fa0", "zf", cols, r, own), ("ga0", "zg", cols, r, own), *x_first])
        task("own y", ["fa0"], [("y0", "yh", cols, r, own)])
        for way, turn in (("f", -1), ("g", 1)):
            for step in range(3):
                index = row_of(turn * sign * (step + 1), yh)
                sends = [(f"{way}a{step + 1}", "z" + way, cols, index, None)] if step < 2 else []
                if way == "f" and step == (1 if FAR[k] else 2):
                    sends.append(("fa3", "zzf" if FAR[k] else "zf", cols, index, None))
                task(f"{way}{step}", [f"{way}a{step}"], [*sends, (f"y{way}{step}", "yh", cols, index, None)])
        task("far", ["fa3"], [("yf3", "yh", cols, row_of(4, yh), None)])
    else:
        beside = [("z+a0", "z+", cols, r, own), ("z-a0", "z-", cols, r, own)]
        task("own", [], [*beside, ("y0", "yh", cols, r, own), *x_first])
        other = row_of(0, 1 - yh)
        task("y", ["y0"], [("z+b0", "z+", cols, other, None), ("z-b0", "z-", cols, other, None)])
        for where, turn, long in (("z+", -1, "a"), ("z-", 1, "b")):
            for which, y in (("a", yh), ("b", 1 - yh)):
                for step in range(3 if which == long and not FAR[k] else 2):
                    index = row_of(turn * (step + 1), y)
                    sends = [(f"{where}{which}{step + 1}", where, cols, index, None)]
                    if which == long and FAR[k] and step == 1:
                        sends.append((f"{where}{which}3", "z" + where, cols, index, None))
                    task(f"{where}{which}{step}", [f"{where}{which}{step}"], sends)
    other = col_of(0, 1 - yl, core)
    task("l", ["yl"], [("x+b0", "x+", rows, other, None), ("x-b0", "x-", rows, other, None), ("k1", "core", rows, other, None)])
    for where, turn, long in (("x+", -1, "a"), ("x-", 1, "b")):
        for which, y in (("a", yl), ("b", 1 - yl)):
            index = col_of(turn, y, core)
            sends = [(f"{where}{which}1", where, rows, index, None)] if which == long else []
            task(f"{where}{which}", [f"{where}{which}0"], [*sends, (f"k{where}{which}0", "core", rows, index, None)])
        index = col_of(2, yl if long == "a" else 1 - yl, core)
        task(f"{where}far", [f"{where}{long}1"], [(f"k{where}far", "core", rows, index, None)])
    return tasks, [f"{message}{k}" for message in messages]


def scatter_tasks(wires, place, k, first_at, second_at, firsts, seconds, coded, codes_in, swapped, swaps_in, store):
    r, c, yh, yl, core, row_of, col_of, _ = place
    size = 16 * SLAB_LANES[k] * 2
    weight = SLAB_LANES[k] / WIDE
    tasks, slots = [], {}

    def term(index):
        return seconds[second_at(index)]

    def arrived(message):
        return decode(codes_in[slots[message]])

    def total(value, needs):
        for need in needs:
            value = value + arrived(need)
        return value

    def send(message, where, value, needs, after=(), rank=0):
        slots[message] = len(slots)

        def body():
            slot = slots[message]
            coded[slot] = encode(total(value(), needs))
            wires.start(f"{message}/{k}", coded.at[slot], codes_in.at[slot], where)

        needed = [f"{need}/{k}" for need in (*needs, *after)] + [f"backward{k}"]
        cost = 0.03 + weight * (0.08 + 0.02 * len(needs))
        tasks.append(Task(f"scatter {message}{k}", needed, cost, body, [(f"{message}/{k}", LINKS[where], size)], rank))

    def keep(name, value, needs, after=()):
        def body():
            store(total(value(), needs))

        needed = [f"{need}/{k}" for need in (*needs, *after)] + [f"backward{k}"]
        tasks.append(Task(f"keep {name}{k}", needed, 0.04 * weight, body, rank=2))

    def of(index):
        return functools.partial(term, index)

    order = [(2, "a"), (2, "b"), (1, "b"), (-1, "a"), (1, "a"), (-1, "b"), (0, "b"), (0, "a")]
    y_of = {"a": yl, "b": 1 - yl}

    def swap_all(some):
        def body():
            for slot in some:
                dx, y = order[slot]
                swapped[slot] = firsts[first_at(col_of(dx, y_of[y], 1 - core))]
                wires.start(f"swap{dx}{y}/{k}", swapped.at[slot], swaps_in.at[slot], "core")

        emits = [(f"swap{order[slot][0]}{order[slot][1]}/{k}", LINKS["core"], 2 * size) for slot in some]
        tasks.append(Task(f"swap{some[0]}{k}", [f"backward{k}"], 0.04 * len(some), body, emits, rank=2))

    def chip_sum(dx, y):
        return firsts[first_at(col_of(dx, y_of[y], core))] + swaps_in[order.index((dx, y))]

    def of_chip(dx, y):
        return functools.partial(chip_sum, dx, y)

    if Z_FIRST[k]:
        sign = place_sign(core)
        spots = {"f3": 4, "f2": 3 * sign, "g2": -3 * sign, "f1": 2 * sign, "g1": -2 * sign, "f0": sign, "g0": -sign, "0": 0}
        for i, (spot, dz) in enumerate(spots.items()):
            send(f"y{spot}", "yh", of(row_of(dz, 1 - yh)), ())
            if i == 1:
                swap_all(range(0, 4))
            if i == 3:
                swap_all(range(4, 8))
        before = {"f3": (), "f2": () if FAR[k] else ("pf3",), "g2": (), "f1": ("pf2", "pf3") if FAR[k] else ("pf2",)}
        before |= {"g1": ("pg2",), "f0": ("pf1",), "g0": ("pg1",)}
        for spot, needs in before.items():
            where = "zzf" if FAR[k] and spot == "f3" else "z" + spot[0]
            send(f"p{spot}", where, of(row_of(spots[spot], yh)), (f"y{spot}", *needs))
        keep("z", of(row_of(0, yh)), ("y0", "pf0", "pg0"))
    else:
        y_row = {"a": yh, "b": 1 - yh}

        def chain(where, turn, which, distance, needs):
            way = "z" + where if FAR[k] and distance == 4 else where
            send(f"p{where}{which}{distance}", way, of(row_of(turn * distance, y_row[which])), needs)

        chain("z+", 1, "a", 4, ())
        chain("z-", -1, "b", 4, ())
        swap_all(range(0, 4))
        chain("z+", 1, "b", 3, ())
        chain("z-", -1, "a", 3, ())
        swap_all(range(4, 8))
        for where, turn, long in (("z+", 1, "a"), ("z-", -1, "b")):
            for which in "ab":
                for distance in range(3 if which == long else 2, 0, -1):
                    needs = [f"p{where}{which}{distance + 1}"]
                    if which == long and FAR[k]:
                        needs = [] if distance == 3 else [*needs, f"p{where}{which}4"] if distance == 2 else needs
                    chain(where, turn, which, distance, needs)
        send("yb", "yh", of(row_of(0, 1 - yh)), ("pz+b1", "pz-b1"))
        keep("z", of(row_of(0, yh)), ("pz+a1", "pz-a1", "yb"))
    send("qx+a2", "x+", of_chip(2, "a"), (), ("swap2a",), 2)
    send("qx-b2", "x-", of_chip(2, "b"), (), ("swap2b",), 2)
    send("qx+b1", "x+", of_chip(1, "b"), (), ("swap1b",), 2)
    send("qx-a1", "x-", of_chip(-1, "a"), (), ("swap-1a",), 2)
    send("qx+a1", "x+", of_chip(1, "a"), ("qx+a2",), ("swap1a",), 2)
    send("qx-b1", "x-", of_chip(-1, "b"), ("qx-b2",), ("swap-1b",), 2)
    send("lb", "yl", of_chip(0, "b"), ("qx+b1", "qx-b1"), ("swap0b",), 2)
    keep("x", of_chip(0, "a"), ("qx+a1", "qx-a1", "lb"), ("swap0a",))
    return tasks


def fold(rho, slab):
    rows = SLAB_ROWS[slab]
    if rows == 16:
        near, far, tail = rho[:, :MAIN], rho[:, MAIN : 2 * MAIN], rho[:, 2 * MAIN :]
    else:
        near, far, tail = rho[:rows, :MAIN], rho[rows:, :MAIN], rho[:rows, MAIN:]
    moved = pltpu.roll(tail, 128 - TAIL, 1)
    even = jnp.concatenate([near + far, tail + moved], axis=1)
    return even, jnp.concatenate([near - far, tail - moved], axis=1)


def exchange_kernel(
    own_in, pair_list_in, pair_count_in, sheet_in, kernel_in, out,
    own, pair_list, pair_count, own_0, own_1, own_2, cols_0, cols_1, cols_2, rows_0, rows_1, rows_2,
    dens_0, dens_1, dens_2, spec_0, spec_1, spec_2, first_0, first_1, first_2,
    second_0, second_1, second_2, coded_0, coded_1, coded_2, codes_in_0, codes_in_1, codes_in_2,
    swapped_0, swapped_1, swapped_2, swaps_in_0, swaps_in_1, swaps_in_2,
    kept_0, kept_1, kept_2, sheet, kernel, send_sem, recv_sem, local_sem,
):
    owns, cols, rows = (own_0, own_1, own_2), (cols_0, cols_1, cols_2), (rows_0, rows_1, rows_2)
    dens, spec = (dens_0, dens_1, dens_2), (spec_0, spec_1, spec_2)
    first_sums, second_sums = (first_0, first_1, first_2), (second_0, second_1, second_2)
    coded, codes_in = (coded_0, coded_1, coded_2), (codes_in_0, codes_in_1, codes_in_2)
    kept = (kept_0, kept_1, kept_2)
    swapped, swaps_in = (swapped_0, swapped_1, swapped_2), (swaps_in_0, swaps_in_1, swaps_in_2)
    place = places()
    r, c, ids = place[0], place[1], place[-1]

    local = [
        pltpu.make_async_copy(sheet_in, sheet, local_sem.at[0]),
        pltpu.make_async_copy(kernel_in, kernel, local_sem.at[1]),
        pltpu.make_async_copy(pair_list_in, pair_list, local_sem.at[2]),
        pltpu.make_async_copy(pair_count_in, pair_count, local_sem.at[3]),
    ]
    greet(ids)
    take = pltpu.make_async_copy(own_in, own, local_sem.at[10])
    take.start()
    take.wait()
    def own_row(x):
        skipped = GX * GX * x % 128
        line = own[:, pl.ds(GX * GX * x - skipped, WIDE)].astype(F32)
        return line[:, skipped : skipped + GX * GX]

    for k in SLABS:
        size = SLAB_ROWS[k]
        band = jnp.concatenate([own_row(x) for x in range(16 * k, 16 * k + size)], axis=0)
        tails = [band[:, MAIN:PART], band[:, PART + MAIN :], jnp.zeros((size, 128 - 2 * TAIL), F32)]
        near, far, tail = band[:, :MAIN], band[:, PART : PART + MAIN], jnp.concatenate(tails, axis=1)
        if size == 16:
            owns[k][...] = jnp.concatenate([near, far, tail], axis=1).astype(BF16)
        else:
            low_rows = jnp.concatenate([far, jnp.zeros((size, 128), F32)], axis=1)
            owns[k][...] = jnp.concatenate([jnp.concatenate([near, tail], axis=1), low_rows], axis=0).astype(BF16)
    met()
    wires = Wires(send_sem, recv_sem, ids)
    keeps = []
    for k in SLABS:
        keeps.append(pltpu.make_async_copy(owns[k], cols[k].at[r], local_sem.at[4 + 2 * k]))
        keeps.append(pltpu.make_async_copy(owns[k], rows[k].at[c], local_sem.at[5 + 2 * k]))

    firsts, seconds, first_band, second_band, before_first, before_second = [], [], [], [], [], []

    def last_slot(bands, wanted):
        at = SLOTS
        for p, band in enumerate(bands):
            at = jnp.where(band == wanted, p, at)
        return at

    def read_pairs():
        count = pair_count[0]
        for p in range(SLOTS):
            first, second = pair_list[0, 0, p], pair_list[0, 1, p]
            other = r * BANDS + first != second * BANDS + c
            firsts.append(first)
            seconds.append(second)
            first_band.append(jnp.where(p < count, first, -1))
            second_band.append(jnp.where((p < count) & other, second, -1))
            before_first.append(last_slot(first_band[:p], first_band[p]))
            before_second.append(last_slot(second_band[:p], second_band[p]))

    def density(k, p):
        return rows[k][firsts[p]].astype(F32) * cols[k][seconds[p]].astype(F32)

    def fill(k, slots):
        size = SLAB_ROWS[k]
        group = 16 // size
        for p in range(slots[0], slots[1], group):
            parts = [fold(density(k, p + i), k) for i in range(group)]
            for parity in range(2):
                value = jnp.concatenate([part[parity] for part in parts], axis=0)
                high, low = split(value)
                dens[k][parity, pl.ds(p * size, 16), :] = high
                dens[k][parity, pl.ds((SLOTS + p) * size, 16), :] = low

    def product(values, parity, at, width):
        lanes = pl.ds(at, width)
        half = values.shape[0] // 2
        wide = jnp.dot(values, sheet[pl.ds(parity * FOLD, FOLD), lanes], preferred_element_type=F32)
        thin = jnp.dot(values[:half], sheet[pl.ds((2 + parity) * FOLD, FOLD), lanes], preferred_element_type=F32)
        return wide[:half] + wide[half:] + thin

    def forward(k, parity, at, width):
        size = SLOTS * SLAB_ROWS[k]
        high, low = split(product(dens[k][parity], parity, at, width))
        lanes = pl.ds(parity * FOLD + at, width)
        spec[k][pl.ds(0, size), lanes] = high
        spec[k][pl.ds(size, size), lanes] = low

    def along():
        return sheet[pl.ds(4 * FOLD, 80), pl.ds(0, 240)]

    def along_x(part):
        high, low = split(part)
        return jnp.dot(along(), jnp.concatenate([high, low, high], axis=0), preferred_element_type=F32)

    def middle(j):
        lanes = pl.ds(j * 256, 256)
        table = kernel[:, lanes]
        for q in range(SLOTS // 2):
            def rows_of(shift):
                return [spec[k][pl.ds((shift * SLOTS + 2 * q) * SLAB_ROWS[k], 2 * SLAB_ROWS[k]), lanes] for k in SLABS]

            high, low = rows_of(0), rows_of(1)
            turned = jnp.dot(along(), jnp.concatenate(high + low + high, axis=0), preferred_element_type=F32)
            high, low = split(along_x(turned * table))
            at = 0
            for k in SLABS:
                size = 2 * SLAB_ROWS[k]
                spec[k][pl.ds(q * size, size), lanes] = high[at : at + size]
                spec[k][pl.ds(SLOTS * SLAB_ROWS[k] + q * size, size), lanes] = low[at : at + size]
                at += size

    def backward(k, at, width):
        size = SLAB_ROWS[k]
        even = product(spec[k][:, pl.ds(0, FOLD)], 0, at, width)
        odd = product(spec[k][:, pl.ds(FOLD, FOLD)], 1, at, width)
        near, far = even + odd, even - odd
        if at == MAIN:
            lane = lax.broadcasted_iota(jnp.int32, near.shape, 1)
            near = jnp.where(lane < TAIL, near, pltpu.roll(far, TAIL, 1))
        for p in range(SLOTS):
            mine = slice(p * size, (p + 1) * size)
            if at == MAIN:
                spans = [(WIDE - 128 if size == 16 else MAIN, near[mine])]
                if size < 16:
                    spans = [(MAIN, jnp.concatenate([near[mine], jnp.zeros_like(near[mine])], axis=0))]
            elif size == 16:
                spans = [(at, near[mine]), (MAIN + at, far[mine])]
            else:
                spans = [(at, jnp.concatenate([near[mine], far[mine]], axis=0))]
            for start, value in spans:
                lanes = pl.ds(start, width)
                to_first = value * cols[k][seconds[p], :, lanes].astype(F32)
                to_second = value * rows[k][firsts[p], :, lanes].astype(F32)
                first_sums[k][p, :, lanes] = to_first + first_sums[k][before_first[p], :, lanes]
                second_sums[k][p, :, lanes] = to_second + second_sums[k][before_second[p], :, lanes]

    stored = set()

    def store(k, value):
        if k not in stored:
            stored.add(k)
            kept[k][...] = value
            return
        value = kept[k][...] + value
        size = SLAB_ROWS[k]
        if size == 16:
            near, far, tail = value[:, :MAIN], value[:, MAIN : 2 * MAIN], value[:, 2 * MAIN :]
        else:
            near, far, tail = value[:size, :MAIN], value[size:, :MAIN], value[:size, MAIN:]
        out[pl.ds(16 * k, size), :] = jnp.concatenate([near, tail[:, :TAIL], far, tail[:, TAIL : 2 * TAIL]], axis=1)

    def begin():
        for copy in local:
            copy.start()
        for copy in keeps:
            copy.start()

    def clear():
        for k in SLABS:
            first_sums[k][SLOTS] = jnp.zeros(first_sums[k].shape[1:], F32)
            second_sums[k][SLOTS] = jnp.zeros(second_sums[k].shape[1:], F32)
        for copy in (*local, *keeps):
            copy.wait()
        read_pairs()

    def nothing():
        pass

    tasks, filled = [], {}
    for k in GATHER_ORDER:
        some, messages = gather_tasks(wires, place, k, owns[k], cols[k], rows[k])
        tasks += some
        filled[k] = messages
    tasks.append(Task("begin", [], 0.1, begin))
    tasks.append(Task("clear", ["begin", "fa10" if Z_FIRST[0] else "z+a10"], 0.5, clear, rank=1))

    def piece(name, needs, cost, body):
        tasks.append(Task(name, needs, cost, body, rank=1))

    turned = []
    for k in GATHER_ORDER:
        weight = SLAB_LANES[k] / WIDE
        for half in range(2):
            piece(f"fill{k}{half}", [*filled[k], "clear"], 0.25 * weight, functools.partial(fill, k, (4 * half, 4 * half + 4)))
        for parity in range(2):
            for at, width in ((0, 512), (512, 384)):
                name = f"forward{k}{parity}{at}"
                turned.append(name)
                piece(name, [f"fill{k}0", f"fill{k}1"], 0.3 * weight, functools.partial(forward, k, parity, at, width))
    def all_middle():
        for j in range(2 * FOLD // 256):
            middle(j)

    piece("middle", turned, 2.5, all_middle)
    for k in SCATTER_ORDER:
        weight = SLAB_LANES[k] / WIDE
        before, names = ["middle"], []
        for at, width in ((0, 256), (256, 256), (512, 256), (768, 128)):
            names.append(f"backward{k}{at}")
            piece(names[-1], before, width / 256 * 0.6 * weight, functools.partial(backward, k, at, width))
        piece(f"backward{k}", names, 0.0, nothing)
        tasks[-1].rank = 0
        tasks += scatter_tasks(
            wires, place, k, functools.partial(last_slot, first_band), functools.partial(last_slot, second_band),
            first_sums[k], second_sums[k], coded[k], codes_in[k], swapped[k], swaps_in[k],
            functools.partial(store, k),
        )
    for task in in_order(tasks)[0]:
        for need in task.needs:
            if need in wires.copies:
                wires.arrive(need)
        task.body()
    for copy in wires.copies.values():
        copy.wait_send()


def exchange(own, pair_list, pair_count):
    vmem = pl.BlockSpec(memory_space=pltpu.VMEM)
    hbm = pl.BlockSpec(memory_space=pltpu.HBM)
    sheet, kernel = (jnp.asarray(t) for t in tables())

    def each(shape, kind):
        return [pltpu.VMEM(shape(k), kind) for k in SLABS]

    def stack(count):
        return lambda k: (count, 16, SLAB_LANES[k])

    return pl.pallas_call(
        exchange_kernel,
        out_shape=jax.ShapeDtypeStruct((GX, GX * GX), F32),
        in_specs=[hbm] * 5,
        out_specs=vmem,
        scratch_shapes=[
            pltpu.VMEM(own.shape, BF16),
            pltpu.SMEM(pair_list.shape, jnp.int32),
            pltpu.SMEM(pair_count.shape, jnp.int32),
            *each(lambda k: (16, SLAB_LANES[k]), BF16),
            *each(stack(BANDS), BF16),
            *each(stack(BANDS), BF16),
            *each(lambda k: (2, 2 * SLOTS * SLAB_ROWS[k], FOLD), BF16),
            *each(lambda k: (2 * SLOTS * SLAB_ROWS[k], 2 * FOLD), BF16),
            *each(stack(SLOTS + 1), F32),
            *each(stack(SLOTS + 1), F32),
            *each(stack(CODED), I16),
            *each(stack(CODED), I16),
            *each(stack(SLOTS), F32),
            *each(stack(SLOTS), F32),
            *each(lambda k: (16, SLAB_LANES[k]), F32),
            pltpu.VMEM(sheet.shape, BF16),
            pltpu.VMEM(kernel.shape, F32),
            pltpu.SemaphoreType.DMA((COPIES,)),
            pltpu.SemaphoreType.DMA((COPIES,)),
            pltpu.SemaphoreType.DMA((11,)),
        ],
        compiler_params=pltpu.CompilerParams(
            collective_id=0, has_side_effects=True, vmem_limit_bytes=62 * 1024 * 1024
        ),
        name="exchange",
    )(own, pair_list, pair_count, sheet, kernel)


def shards(orbitals, pair_list, pair_count):
    fields = exchange(orbitals, jnp.swapaxes(pair_list, 1, 2), pair_count)
    return fields.reshape(1, GX * GX * GX)


def solution(mesh):
    return jax.shard_map(
        shards,
        mesh=mesh,
        in_specs=(P(("row", "col"), None), P(("row", "col"), None, None), P(("row", "col"))),
        out_specs=P(("row", "col"), None),
        check_vma=False,
    )
```

```python
import functools

import jax
import jax.numpy as jnp
import ml_dtypes
import numpy as np
from jax import lax
from jax.experimental import pallas as pl
from jax.experimental.pallas import tpu as pltpu
from jax.sharding import PartitionSpec as P

GX = 40
HALF = GX // 2
PART = HALF * GX
MAIN = 768
TAIL = PART - MAIN
WIDE = 2 * MAIN + 128
FOLD = MAIN + 128
SLOTS = 8
BANDS = 16
NZ, NX = 8, 4
SLAB_ROWS = (16, 16, 8)
SLAB_LANES = (WIDE, WIDE, FOLD)
SLABS = range(3)
screen_width = 0.9
MESH = pl.DeviceIdType.MESH
F32, BF16, I16 = jnp.float32, jnp.bfloat16, jnp.int16
TOP = 32767.0
Z_FIRST = (True, False, False)
FAR = (True, False, False)
GATHER_ORDER = (2, 0, 1)
SCATTER_ORDER = (1, 2, 0)
FORWARD_GROUPS = ((0,), (1,), (2,))
BACKWARD_GROUPS = ((1,), (2, 0))
COPIES = 192
CODED = 22
GREETED = ("z+", "z-", "zz+", "zz-", "yh", "x+", "x-", "yl", "core")


def split_np(a):
    high = a.astype(ml_dtypes.bfloat16)
    low = (a - high.astype(np.float64)).astype(ml_dtypes.bfloat16)
    return high, low


@functools.cache
def tables():
    def cas(phase):
        return np.cos(phase) + np.sin(phase)

    n, h = np.arange(GX), np.arange(HALF)
    root = 1.0 / np.sqrt(GX)
    full = cas(2.0 * np.pi * np.outer(n, n) / GX) * root
    even = cas(2.0 * np.pi * np.outer(h, h) / HALF) * root
    odd = cas(2.0 * np.pi * np.outer(2 * h + 1, 2 * h + 1) / (4 * HALF)) * root
    plane = np.zeros((2, FOLD, FOLD))
    plane[0, :PART, :PART] = np.kron(even, full)
    plane[1, :PART, :PART] = np.kron(odd, full)
    plane_high, plane_low = split_np(plane)
    xs = np.concatenate([np.r_[a:b, a:b] for a, b in ((0, 16), (16, 32), (32, 40))])
    pair = np.concatenate([np.r_[[0] * k, [1] * k] for k in (16, 16, 8)])
    both = np.where(pair[:, None] == pair[None, :], full[xs][:, xs], 0.0)
    high, low = split_np(both)
    along = np.concatenate([high, high, low], axis=1)
    signed = np.where(n < GX // 2, n, n - GX) * (2.0 * np.pi / GX)
    squared = signed**2
    total = squared[:, None, None] + squared[None, :, None] + squared[None, None, :]
    safe = np.where(total > 0, total, 1.0)
    screened = 4.0 * np.pi * (1.0 - np.exp(-safe / (4.0 * screen_width**2))) / safe
    kernel = np.where(total > 0, screened, np.pi / screen_width**2)
    padded = np.zeros((GX, 2, FOLD), np.float32)
    padded[:, 0, :PART] = kernel[:, 0::2].reshape(GX, PART)
    padded[:, 1, :PART] = kernel[:, 1::2].reshape(GX, PART)
    sheet = np.zeros((4 * FOLD + 80, FOLD), ml_dtypes.bfloat16)
    sheet[: 2 * FOLD] = plane_high.reshape(2 * FOLD, FOLD)
    sheet[2 * FOLD : 4 * FOLD] = plane_low.reshape(2 * FOLD, FOLD)
    sheet[4 * FOLD :, :240] = along
    return sheet, padded.reshape(GX, 2 * FOLD)[xs]


def group_rows(group):
    return sum(SLOTS * SLAB_ROWS[k] for k in group)


def spot_of(groups, k):
    for g, group in enumerate(groups):
        if k in group:
            return g, group_rows(group[: group.index(k)]), group_rows(group)


def split(x):
    high = x.astype(BF16)
    return high, (x - high.astype(F32)).astype(BF16)


def encode(value):
    most = jnp.max(jnp.abs(value), axis=1, keepdims=True)
    power = jnp.floor(jnp.log(jnp.maximum(most, 1e-30)) * 1.4426950408889634)
    share = value * (0.5 * jnp.exp2(-power))
    root = share * lax.rsqrt(jnp.maximum(jnp.abs(share), 1e-20))
    code = jnp.clip(jnp.round(root * TOP), -TOP, TOP)
    lanes = lax.broadcasted_iota(jnp.int32, (value.shape[0], 128), 1)
    last = jnp.where(lanes >= 64, power, code[:, -128:])
    return jnp.concatenate([code[:, :-128], last], axis=1).astype(jnp.int32).astype(I16)


def decode(code):
    wide = code.astype(jnp.int32).astype(F32)
    scale = jnp.exp2(wide[:, -64:-63]) * (2.0 / (TOP * TOP))
    return wide * jnp.abs(wide) * scale


def places():
    r, c = lax.axis_index("row"), lax.axis_index("col")
    z, yh = r // 2, r % 2
    x, yl, core = c // 4, (c // 2) % 2, c % 2

    def row_of(dz, y):
        return ((z + dz + NZ) % NZ) * 2 + y

    def col_of(dx, y, k):
        return ((x + dx + NX) % NX) * 4 + y * 2 + k

    ids = {
        "z+": (row_of(1, yh), c),
        "z-": (row_of(-1, yh), c),
        "zf": (row_of(1 - 2 * core, yh), c),
        "zg": (row_of(2 * core - 1, yh), c),
        "zz+": (row_of(2, yh), c),
        "zz-": (row_of(-2, yh), c),
        "zzf": (row_of(2 - 4 * core, yh), c),
        "yh": (row_of(0, 1 - yh), c),
        "x+": (r, col_of(1, yl, core)),
        "x-": (r, col_of(-1, yl, core)),
        "yl": (r, col_of(0, 1 - yl, core)),
        "core": (r, col_of(0, yl, 1 - core)),
    }
    return r, c, yh, yl, core, row_of, col_of, ids


def place_sign(core):
    return 1 - 2 * core


def greet(ids):
    barrier = pltpu.get_barrier_semaphore()
    for where in GREETED:
        pl.semaphore_signal(barrier, inc=1, device_id=ids[where], device_id_type=MESH)


def met():
    pl.semaphore_wait(pltpu.get_barrier_semaphore(), len(GREETED))


class Wires:
    def __init__(self, send_sem, recv_sem, ids):
        self.send_sem, self.recv_sem, self.ids = send_sem, recv_sem, ids
        self.copies, self.waited = {}, set()

    def start(self, name, source, target, where):
        at = len(self.copies)
        copy = pltpu.make_async_remote_copy(
            src_ref=source,
            dst_ref=target,
            send_sem=self.send_sem.at[at],
            recv_sem=self.recv_sem.at[at],
            device_id=self.ids[where],
            device_id_type=MESH,
        )
        copy.start()
        self.copies[name] = copy

    def arrive(self, name):
        if name not in self.waited:
            self.waited.add(name)
            self.copies[name].wait_recv()


RATES = {"z": 1 / 49e3, "x": 1 / 49e3, "y": 1 / 49e3, "l": 1 / 49e3, "c": 1 / 400e3}
DELAYS = {'z': 3.6, 'x': 3.2, 'y': 3.8, 'l': 3.2, 'c': 0.8}


class Task:
    def __init__(self, name, needs, cost, body, emits=(), rank=0):
        self.name, self.needs, self.cost, self.body = name, list(needs), cost, body
        self.emits, self.rank = list(emits), rank


def in_order(tasks):
    known, free, left, order, now = {}, {}, list(tasks), [], 0.0
    while left:
        ready = []
        for i, task in enumerate(left):
            if all(need in known for need in task.needs):
                at = max([known[need] for need in task.needs], default=0.0)
                ready.append((max(at, now), task.rank, at, i))
        at, _, _, i = min(ready)
        task = left.pop(i)
        now = at + task.cost
        known[task.name] = now
        for message, (link, hops), size in task.emits:
            time = size * RATES[link[0]]
            begin = max(now, free.get(link, 0.0))
            free[link] = begin + time * hops
            known[message] = begin + time + DELAYS[link[0]] + 1.0 * (hops - 1)
        task.needs.sort(key=known.get)
        order.append(task)
    return order, now


LINKS = {
    "z+": ("z+", 1), "z-": ("z-", 1), "zf": ("z+", 1), "zg": ("z-", 1), "zz+": ("z+", 2), "zz-": ("z-", 2), "zzf": ("z+", 2),
    "x+": ("x+", 1), "x-": ("x-", 1), "yh": ("y", 1), "yl": ("l", 1), "core": ("c", 1),
}


def gather_tasks(wires, place, k, own, cols, rows):
    r, c, yh, yl, core, row_of, col_of, _ = place
    size = 16 * SLAB_LANES[k] * 2
    tasks = []
    messages = []

    def task(name, needs, sends):
        def body():
            for message, where, block, index, source in sends:
                target = block.at[index]
                wires.start(f"{message}{k}", target if source is None else source, target, where)

        emits = [(f"{send[0]}{k}", LINKS[send[1]], size) for send in sends]
        messages.extend(send[0] for send in sends)
        tasks.append(Task(f"gather {name}{k}", [f"{need}{k}" for need in needs], 0.03 * len(sends), body, emits))

    x_first = [("x+a0", "x+", rows, c, own), ("x-a0", "x-", rows, c, own), ("yl", "yl", rows, c, own), ("k0", "core", rows, c, own)]
    if Z_FIRST[k]:
        sign = place_sign(core)
        task("own", [], [("fa0", "zf", cols, r, own), ("ga0", "zg", cols, r, own), *x_first])
        task("own y", ["fa0"], [("y0", "yh", cols, r, own)])
        for way, turn in (("f", -1), ("g", 1)):
            for step in range(3):
                index = row_of(turn * sign * (step + 1), yh)
                sends = [(f"{way}a{step + 1}", "z" + way, cols, index, None)] if step < 2 else []
                if way == "f" and step == (1 if FAR[k] else 2):
                    sends.append(("fa3", "zzf" if FAR[k] else "zf", cols, index, None))
                task(f"{way}{step}", [f"{way}a{step}"], [*sends, (f"y{way}{step}", "yh", cols, index, None)])
        task("far", ["fa3"], [("yf3", "yh", cols, row_of(4, yh), None)])
    else:
        beside = [("z+a0", "z+", cols, r, own), ("z-a0", "z-", cols, r, own)]
        task("own", [], [*beside, ("y0", "yh", cols, r, own), *x_first])
        other = row_of(0, 1 - yh)
        task("y", ["y0"], [("z+b0", "z+", cols, other, None), ("z-b0", "z-", cols, other, None)])
        for where, turn, long in (("z+", -1, "a"), ("z-", 1, "b")):
            for which, y in (("a", yh), ("b", 1 - yh)):
                for step in range(3 if which == long and not FAR[k] else 2):
                    index = row_of(turn * (step + 1), y)
                    sends = [(f"{where}{which}{step + 1}", where, cols, index, None)]
                    if which == long and FAR[k] and step == 1:
                        sends.append((f"{where}{which}3", "z" + where, cols, index, None))
                    task(f"{where}{which}{step}", [f"{where}{which}{step}"], sends)
    other = col_of(0, 1 - yl, core)
    task("l", ["yl"], [("x+b0", "x+", rows, other, None), ("x-b0", "x-", rows, other, None), ("k1", "core", rows, other, None)])
    for where, turn, long in (("x+", -1, "a"), ("x-", 1, "b")):
        for which, y in (("a", yl), ("b", 1 - yl)):
            index = col_of(turn, y, core)
            sends = [(f"{where}{which}1", where, rows, index, None)] if which == long else []
            task(f"{where}{which}", [f"{where}{which}0"], [*sends, (f"k{where}{which}0", "core", rows, index, None)])
        index = col_of(2, yl if long == "a" else 1 - yl, core)
        task(f"{where}far", [f"{where}{long}1"], [(f"k{where}far", "core", rows, index, None)])
    return tasks, [f"{message}{k}" for message in messages]


def scatter_tasks(wires, place, k, first_at, second_at, firsts, seconds, coded, codes_in, swapped, swaps_in, store):
    r, c, yh, yl, core, row_of, col_of, _ = place
    size = 16 * SLAB_LANES[k] * 2
    weight = SLAB_LANES[k] / WIDE
    tasks, slots = [], {}

    def term(index):
        return seconds[second_at(index)]

    def arrived(message):
        return decode(codes_in[slots[message]])

    def total(value, needs):
        for need in needs:
            value = value + arrived(need)
        return value

    def send(message, where, value, needs, after=(), rank=0):
        slots[message] = len(slots)

        def body():
            slot = slots[message]
            coded[slot] = encode(total(value(), needs))
            wires.start(f"{message}/{k}", coded.at[slot], codes_in.at[slot], where)

        needed = [f"{need}/{k}" for need in (*needs, *after)] + [f"backward{k}"]
        cost = 0.03 + weight * (0.08 + 0.02 * len(needs))
        tasks.append(Task(f"scatter {message}{k}", needed, cost, body, [(f"{message}/{k}", LINKS[where], size)], rank))

    def keep(name, value, needs, after=()):
        def body():
            store(total(value(), needs))

        needed = [f"{need}/{k}" for need in (*needs, *after)] + [f"backward{k}"]
        tasks.append(Task(f"keep {name}{k}", needed, 0.04 * weight, body, rank=2))

    def of(index):
        return functools.partial(term, index)

    order = [(2, "a"), (2, "b"), (1, "b"), (-1, "a"), (1, "a"), (-1, "b"), (0, "b"), (0, "a")]
    y_of = {"a": yl, "b": 1 - yl}

    def swap_all(some):
        def body():
            for slot in some:
                dx, y = order[slot]
                swapped[slot] = firsts[first_at(col_of(dx, y_of[y], 1 - core))]
                wires.start(f"swap{dx}{y}/{k}", swapped.at[slot], swaps_in.at[slot], "core")

        emits = [(f"swap{order[slot][0]}{order[slot][1]}/{k}", LINKS["core"], 2 * size) for slot in some]
        tasks.append(Task(f"swap{some[0]}{k}", [f"backward{k}"], 0.04 * len(some), body, emits, rank=2))

    def chip_sum(dx, y):
        return firsts[first_at(col_of(dx, y_of[y], core))] + swaps_in[order.index((dx, y))]

    def of_chip(dx, y):
        return functools.partial(chip_sum, dx, y)

    if Z_FIRST[k]:
        sign = place_sign(core)
        spots = {"f3": 4, "f2": 3 * sign, "g2": -3 * sign, "f1": 2 * sign, "g1": -2 * sign, "f0": sign, "g0": -sign, "0": 0}
        for i, (spot, dz) in enumerate(spots.items()):
            send(f"y{spot}", "yh", of(row_of(dz, 1 - yh)), ())
            if i == 1:
                swap_all(range(0, 4))
            if i == 3:
                swap_all(range(4, 8))
        before = {"f3": (), "f2": () if FAR[k] else ("pf3",), "g2": (), "f1": ("pf2", "pf3") if FAR[k] else ("pf2",)}
        before |= {"g1": ("pg2",), "f0": ("pf1",), "g0": ("pg1",)}
        for spot, needs in before.items():
            where = "zzf" if FAR[k] and spot == "f3" else "z" + spot[0]
            send(f"p{spot}", where, of(row_of(spots[spot], yh)), (f"y{spot}", *needs))
        keep("z", of(row_of(0, yh)), ("y0", "pf0", "pg0"))
    else:
        y_row = {"a": yh, "b": 1 - yh}

        def chain(where, turn, which, distance, needs):
            way = "z" + where if FAR[k] and distance == 4 else where
            send(f"p{where}{which}{distance}", way, of(row_of(turn * distance, y_row[which])), needs)

        chain("z+", 1, "a", 4, ())
        chain("z-", -1, "b", 4, ())
        swap_all(range(0, 4))
        chain("z+", 1, "b", 3, ())
        chain("z-", -1, "a", 3, ())
        swap_all(range(4, 8))
        for where, turn, long in (("z+", 1, "a"), ("z-", -1, "b")):
            for which in "ab":
                for distance in range(3 if which == long else 2, 0, -1):
                    needs = [f"p{where}{which}{distance + 1}"]
                    if which == long and FAR[k]:
                        needs = [] if distance == 3 else [*needs, f"p{where}{which}4"] if distance == 2 else needs
                    chain(where, turn, which, distance, needs)
        send("yb", "yh", of(row_of(0, 1 - yh)), ("pz+b1", "pz-b1"))
        keep("z", of(row_of(0, yh)), ("pz+a1", "pz-a1", "yb"))
    send("qx+a2", "x+", of_chip(2, "a"), (), ("swap2a",), 2)
    send("qx-b2", "x-", of_chip(2, "b"), (), ("swap2b",), 2)
    send("qx+b1", "x+", of_chip(1, "b"), (), ("swap1b",), 2)
    send("qx-a1", "x-", of_chip(-1, "a"), (), ("swap-1a",), 2)
    send("qx+a1", "x+", of_chip(1, "a"), ("qx+a2",), ("swap1a",), 2)
    send("qx-b1", "x-", of_chip(-1, "b"), ("qx-b2",), ("swap-1b",), 2)
    send("lb", "yl", of_chip(0, "b"), ("qx+b1", "qx-b1"), ("swap0b",), 2)
    keep("x", of_chip(0, "a"), ("qx+a1", "qx-a1", "lb"), ("swap0a",))
    return tasks


def fold(rho, slab):
    rows = SLAB_ROWS[slab]
    if rows == 16:
        near, far, tail = rho[:, :MAIN], rho[:, MAIN : 2 * MAIN], rho[:, 2 * MAIN :]
    else:
        near, far, tail = rho[:rows, :MAIN], rho[rows:, :MAIN], rho[:rows, MAIN:]
    moved = pltpu.roll(tail, 128 - TAIL, 1)
    even = jnp.concatenate([near + far, tail + moved], axis=1)
    return even, jnp.concatenate([near - far, tail - moved], axis=1)


def exchange_kernel(
    own_in, pair_list_in, pair_count_in, sheet_in, kernel_in, out,
    own, pair_list, pair_count, own_0, own_1, own_2, cols_0, cols_1, cols_2, rows_0, rows_1, rows_2,
    dens, spec, first_0, first_1, first_2,
    second_0, second_1, second_2, coded_0, coded_1, coded_2, codes_in_0, codes_in_1, codes_in_2,
    swapped_0, swapped_1, swapped_2, swaps_in_0, swaps_in_1, swaps_in_2,
    kept_0, kept_1, kept_2, sheet, kernel, send_sem, recv_sem, local_sem,
):
    owns, cols, rows = (own_0, own_1, own_2), (cols_0, cols_1, cols_2), (rows_0, rows_1, rows_2)
    first_sums, second_sums = (first_0, first_1, first_2), (second_0, second_1, second_2)
    coded, codes_in = (coded_0, coded_1, coded_2), (codes_in_0, codes_in_1, codes_in_2)
    kept = (kept_0, kept_1, kept_2)
    swapped, swaps_in = (swapped_0, swapped_1, swapped_2), (swaps_in_0, swaps_in_1, swaps_in_2)
    place = places()
    r, c, ids = place[0], place[1], place[-1]

    local = [
        pltpu.make_async_copy(sheet_in, sheet, local_sem.at[0]),
        pltpu.make_async_copy(kernel_in, kernel, local_sem.at[1]),
        pltpu.make_async_copy(pair_list_in, pair_list, local_sem.at[2]),
        pltpu.make_async_copy(pair_count_in, pair_count, local_sem.at[3]),
    ]
    greet(ids)
    take = pltpu.make_async_copy(own_in, own, local_sem.at[10])
    take.start()
    take.wait()
    def own_row(x):
        skipped = GX * GX * x % 128
        line = own[:, pl.ds(GX * GX * x - skipped, WIDE)].astype(F32)
        return line[:, skipped : skipped + GX * GX]

    for k in SLABS:
        size = SLAB_ROWS[k]
        band = jnp.concatenate([own_row(x) for x in range(16 * k, 16 * k + size)], axis=0)
        tails = [band[:, MAIN:PART], band[:, PART + MAIN :], jnp.zeros((size, 128 - 2 * TAIL), F32)]
        near, far, tail = band[:, :MAIN], band[:, PART : PART + MAIN], jnp.concatenate(tails, axis=1)
        if size == 16:
            owns[k][...] = jnp.concatenate([near, far, tail], axis=1).astype(BF16)
        else:
            low_rows = jnp.concatenate([far, jnp.zeros((size, 128), F32)], axis=1)
            owns[k][...] = jnp.concatenate([jnp.concatenate([near, tail], axis=1), low_rows], axis=0).astype(BF16)
    met()
    wires = Wires(send_sem, recv_sem, ids)
    keeps = []
    for k in SLABS:
        keeps.append(pltpu.make_async_copy(owns[k], cols[k].at[r], local_sem.at[4 + 2 * k]))
        keeps.append(pltpu.make_async_copy(owns[k], rows[k].at[c], local_sem.at[5 + 2 * k]))

    firsts, seconds, first_band, second_band, before_first, before_second = [], [], [], [], [], []

    def last_slot(bands, wanted):
        at = SLOTS
        for p, band in enumerate(bands):
            at = jnp.where(band == wanted, p, at)
        return at

    def read_pairs():
        count = pair_count[0]
        for p in range(SLOTS):
            first, second = pair_list[0, 0, p], pair_list[0, 1, p]
            other = r * BANDS + first != second * BANDS + c
            firsts.append(first)
            seconds.append(second)
            first_band.append(jnp.where(p < count, first, -1))
            second_band.append(jnp.where((p < count) & other, second, -1))
            before_first.append(last_slot(first_band[:p], first_band[p]))
            before_second.append(last_slot(second_band[:p], second_band[p]))

    def density(k, p):
        return rows[k][firsts[p]].astype(F32) * cols[k][seconds[p]].astype(F32)

    def fill(k, slots):
        size = SLAB_ROWS[k]
        group = 16 // size
        g, base, total = spot_of(FORWARD_GROUPS, k)
        for p in range(slots[0], slots[1], group):
            parts = [fold(density(k, p + i), k) for i in range(group)]
            for parity in range(2):
                value = jnp.concatenate([part[parity] for part in parts], axis=0)
                high, low = split(value)
                dens[g][parity, pl.ds(base + p * size, 16), :] = high
                dens[g][parity, pl.ds(total + base + p * size, 16), :] = low

    def product(values, parity, at, width):
        lanes = pl.ds(at, width)
        half = values.shape[0] // 2
        wide = jnp.dot(values, sheet[pl.ds(parity * FOLD, FOLD), lanes], preferred_element_type=F32)
        thin = jnp.dot(values[:half], sheet[pl.ds((2 + parity) * FOLD, FOLD), lanes], preferred_element_type=F32)
        return wide[:half] + wide[half:] + thin

    def forward(g, parity, at, width):
        high, low = split(product(dens[g][parity], parity, at, width))
        lanes = pl.ds(parity * FOLD + at, width)
        for k in FORWARD_GROUPS[g]:
            start, size = spot_of(FORWARD_GROUPS, k)[1], SLOTS * SLAB_ROWS[k]
            b, base, total = spot_of(BACKWARD_GROUPS, k)
            spec[b][pl.ds(base, size), lanes] = high[start : start + size]
            spec[b][pl.ds(total + base, size), lanes] = low[start : start + size]

    def along():
        return sheet[pl.ds(4 * FOLD, 80), pl.ds(0, 240)]

    def along_x(part):
        high, low = split(part)
        return jnp.dot(along(), jnp.concatenate([high, low, high], axis=0), preferred_element_type=F32)

    def middle(j):
        lanes = pl.ds(j * 256, 256)
        table = kernel[:, lanes]
        for q in range(SLOTS // 2):
            def place_of(k, shift):
                b, base, total = spot_of(BACKWARD_GROUPS, k)
                return b, pl.ds(base + shift * total + 2 * q * SLAB_ROWS[k], 2 * SLAB_ROWS[k])

            def rows_of(shift):
                spots = [place_of(k, shift) for k in SLABS]
                return [spec[b][some, lanes] for b, some in spots]

            high, low = rows_of(0), rows_of(1)
            turned = jnp.dot(along(), jnp.concatenate(high + low + high, axis=0), preferred_element_type=F32)
            high, low = split(along_x(turned * table))
            at = 0
            for k in SLABS:
                size = 2 * SLAB_ROWS[k]
                for shift, part in enumerate((high, low)):
                    b, some = place_of(k, shift)
                    spec[b][some, lanes] = part[at : at + size]
                at += size

    def backward(b, at, width):
        even = product(spec[b][:, pl.ds(0, FOLD)], 0, at, width)
        odd = product(spec[b][:, pl.ds(FOLD, FOLD)], 1, at, width)
        near, far = even + odd, even - odd
        if at == MAIN:
            lane = lax.broadcasted_iota(jnp.int32, near.shape, 1)
            near = jnp.where(lane < TAIL, near, pltpu.roll(far, TAIL, 1))
        for k in BACKWARD_GROUPS[b]:
            add_terms(k, near, far, spot_of(BACKWARD_GROUPS, k)[1], at, width)

    def add_terms(k, near, far, base, at, width):
        size = SLAB_ROWS[k]
        for p in range(SLOTS):
            mine = slice(base + p * size, base + (p + 1) * size)
            if at == MAIN:
                spans = [(WIDE - 128 if size == 16 else MAIN, near[mine])]
                if size < 16:
                    spans = [(MAIN, jnp.concatenate([near[mine], jnp.zeros_like(near[mine])], axis=0))]
            elif size == 16:
                spans = [(at, near[mine]), (MAIN + at, far[mine])]
            else:
                spans = [(at, jnp.concatenate([near[mine], far[mine]], axis=0))]
            for start, value in spans:
                lanes = pl.ds(start, width)
                to_first = value * cols[k][seconds[p], :, lanes].astype(F32)
                to_second = value * rows[k][firsts[p], :, lanes].astype(F32)
                first_sums[k][p, :, lanes] = to_first + first_sums[k][before_first[p], :, lanes]
                second_sums[k][p, :, lanes] = to_second + second_sums[k][before_second[p], :, lanes]

    stored = set()

    def store(k, value):
        if k not in stored:
            stored.add(k)
            kept[k][...] = value
            return
        value = kept[k][...] + value
        size = SLAB_ROWS[k]
        if size == 16:
            near, far, tail = value[:, :MAIN], value[:, MAIN : 2 * MAIN], value[:, 2 * MAIN :]
        else:
            near, far, tail = value[:size, :MAIN], value[size:, :MAIN], value[:size, MAIN:]
        out[pl.ds(16 * k, size), :] = jnp.concatenate([near, tail[:, :TAIL], far, tail[:, TAIL : 2 * TAIL]], axis=1)

    def begin():
        for copy in local:
            copy.start()
        for copy in keeps:
            copy.start()

    def clear():
        for k in SLABS:
            first_sums[k][SLOTS] = jnp.zeros(first_sums[k].shape[1:], F32)
            second_sums[k][SLOTS] = jnp.zeros(second_sums[k].shape[1:], F32)
        for copy in (*local, *keeps):
            copy.wait()
        read_pairs()

    def nothing():
        pass

    tasks, filled = [], {}
    for k in GATHER_ORDER:
        some, messages = gather_tasks(wires, place, k, owns[k], cols[k], rows[k])
        tasks += some
        filled[k] = messages
    tasks.append(Task("begin", [], 0.1, begin))
    tasks.append(Task("clear", ["begin", "fa10" if Z_FIRST[0] else "z+a10"], 0.5, clear, rank=1))

    def piece(name, needs, cost, body):
        tasks.append(Task(name, needs, cost, body, rank=1))

    turned = []
    for k in GATHER_ORDER:
        weight = SLAB_LANES[k] / WIDE
        for half in range(2):
            piece(f"fill{k}{half}", [*filled[k], "clear"], 0.25 * weight, functools.partial(fill, k, (4 * half, 4 * half + 4)))
    for g, group in enumerate(FORWARD_GROUPS):
        ready = [f"fill{k}{half}" for k in group for half in range(2)]
        for parity in range(2):
            for at, width in ((0, 512), (512, 384)):
                name = f"forward{g}{parity}{at}"
                turned.append(name)
                cost = 0.12 + 0.18 * group_rows(group) / 128
                piece(name, ready, cost, functools.partial(forward, g, parity, at, width))

    def all_middle():
        for j in range(2 * FOLD // 256):
            middle(j)

    piece("middle", turned, 2.5, all_middle)
    for b, group in enumerate(BACKWARD_GROUPS):
        names = []
        for at, width in ((0, 256), (256, 256), (512, 256), (768, 128)):
            names.append(f"backward of {b}{at}")
            cost = width / 256 * (0.3 + 0.3 * group_rows(group) / 128)
            piece(names[-1], ["middle"], cost, functools.partial(backward, b, at, width))
        for k in group:
            tasks.append(Task(f"backward{k}", names, 0.0, nothing))
    for k in SCATTER_ORDER:
        tasks += scatter_tasks(
            wires, place, k, functools.partial(last_slot, first_band), functools.partial(last_slot, second_band),
            first_sums[k], second_sums[k], coded[k], codes_in[k], swapped[k], swaps_in[k],
            functools.partial(store, k),
        )
    for task in in_order(tasks)[0]:
        for need in task.needs:
            if need in wires.copies:
                wires.arrive(need)
        task.body()
    for copy in wires.copies.values():
        copy.wait_send()


def exchange(own, pair_list, pair_count):
    vmem = pl.BlockSpec(memory_space=pltpu.VMEM)
    hbm = pl.BlockSpec(memory_space=pltpu.HBM)
    sheet, kernel = (jnp.asarray(t) for t in tables())

    def each(shape, kind):
        return [pltpu.VMEM(shape(k), kind) for k in SLABS]

    def stack(count):
        return lambda k: (count, 16, SLAB_LANES[k])

    return pl.pallas_call(
        exchange_kernel,
        out_shape=jax.ShapeDtypeStruct((GX, GX * GX), F32),
        in_specs=[hbm] * 5,
        out_specs=vmem,
        scratch_shapes=[
            pltpu.VMEM(own.shape, BF16),
            pltpu.SMEM(pair_list.shape, jnp.int32),
            pltpu.SMEM(pair_count.shape, jnp.int32),
            *each(lambda k: (16, SLAB_LANES[k]), BF16),
            *each(stack(BANDS), BF16),
            *each(stack(BANDS), BF16),
            [pltpu.VMEM((2, 2 * group_rows(group), FOLD), BF16) for group in FORWARD_GROUPS],
            [pltpu.VMEM((2 * group_rows(group), 2 * FOLD), BF16) for group in BACKWARD_GROUPS],
            *each(stack(SLOTS + 1), F32),
            *each(stack(SLOTS + 1), F32),
            *each(stack(CODED), I16),
            *each(stack(CODED), I16),
            *each(stack(SLOTS), F32),
            *each(stack(SLOTS), F32),
            *each(lambda k: (16, SLAB_LANES[k]), F32),
            pltpu.VMEM(sheet.shape, BF16),
            pltpu.VMEM(kernel.shape, F32),
            pltpu.SemaphoreType.DMA((COPIES,)),
            pltpu.SemaphoreType.DMA((COPIES,)),
            pltpu.SemaphoreType.DMA((11,)),
        ],
        compiler_params=pltpu.CompilerParams(
            collective_id=0, has_side_effects=True, vmem_limit_bytes=62 * 1024 * 1024
        ),
        name="exchange",
    )(own, pair_list, pair_count, sheet, kernel)


def shards(orbitals, pair_list, pair_count):
    fields = exchange(orbitals, jnp.swapaxes(pair_list, 1, 2), pair_count)
    return fields.reshape(1, GX * GX * GX)


def solution(mesh):
    return jax.shard_map(
        shards,
        mesh=mesh,
        in_specs=(P(("row", "col"), None), P(("row", "col"), None, None), P(("row", "col"))),
        out_specs=P(("row", "col"), None),
        check_vma=False,
    )
```
